32 devices in a mesh: parts: 2 (over y), expert: 4 (over z), dp: 4 (over x, core), sub: 1.
Axes of the slice: x: 2, y: 2, z: 4, core: 2. Of those that a mesh axis runs over, the one named last changes fastest.
Arguments:
- tokens: bfloat16 [4096, 1024], P(('parts', 'expert', 'dp', 'sub')), parts along dimension 0, may hold values from -6 to 6
- expert_choice: int32 [4096, 1], P(('parts', 'expert', 'dp', 'sub')), parts along dimension 0, may hold values from 0 to 3; in each aligned block of 128 rows (0 to 127, 128 to 255, ...) at most 48 rows name the same one
- gate_prob: float32 [4096, 1], P(('parts', 'expert', 'dp', 'sub')), parts along dimension 0, may hold values from 0.1 to 1
- cotangent: bfloat16 [4096, 1024], P(('parts', 'expert', 'dp', 'sub')), parts along dimension 0, may hold values from -6 to 6
- w_gate: bfloat16 [4, 768, 1024], P('expert', 'sub'), may hold values from -0.1875 to 0.1875
- w_up: bfloat16 [4, 768, 1024], P('expert', 'sub'), may hold values from -0.1875 to 0.1875
- w_down: bfloat16 [4, 768, 1024], P('expert', 'sub'), may hold values from -0.21875 to 0.21875
Outputs:
- layer_out: bfloat16 [4096, 1024], P(('parts', 'expert', 'dp', 'sub')), parts along dimension 0
- d_tokens: bfloat16 [4096, 1024], P(('parts', 'expert', 'dp', 'sub')), parts along dimension 0
- d_gate: float32 [4096, 1], P(('parts', 'expert', 'dp', 'sub')), parts along dimension 0
- d_w_gate: bfloat16 [8, 768, 1024], P(('parts', 'expert'), 'sub', 'dp'), parts along dimension 0
- d_w_up: bfloat16 [8, 768, 1024], P(('parts', 'expert'), 'sub', 'dp'), parts along dimension 0
- d_w_down: bfloat16 [8, 768, 1024], P(('parts', 'expert'), 'sub', 'dp'), parts along dimension 0
The draws below stay inside these ranges and needn't reach their ends.
There are 2 independent parts, one for each index of `parts`. The reference program is written for one: setup_inputs(seed, part) draws one part's arguments, and reference() takes and returns one part's arrays. A program takes and returns all parts, laid end to end along the dimension named above; an argument that names none is the same for every part. Nothing has to cross between parts.
Inputs may be any that keep to these rules, and one draw needn't show every extreme that they name: `expert_choice`: each row names one expert. Within the tokens of one device (aligned blocks of 128 rows), no expert is named by more than 48 rows, and in every draw some expert is named by exactly 48 rows of some block.
All inputs are finite; a program needn't handle non-finite values.
Results may differ from the reference program's by a relative error of at most 0.017.
Values may be sent and summed in bfloat16 or wider, within the bound.
A program may use at most 64 MiB of HBM per device.

```python
import math
import jax
import jax.numpy as jnp
import numpy as np
from jax import lax

D = 1024
FF = 768
TOK_DEV = 128
TOP = 1
EXPERTS = 4
CAP = 48
HID_PARTS = 1
TOKENS = 2048
N_EXPERT = 4
N_DP = 4
N_SUB = 1


def level_of(key, dims, cuts, smallest, high):
    def one(dim, blocks):
        steps = jax.random.uniform(jax.random.fold_in(jax.random.fold_in(key, 6), dim), (blocks,), jnp.float32, smallest / len(cuts), high / len(cuts))
        return jnp.repeat(jnp.exp(steps), dims[dim] // blocks).reshape((-1,) + (1,) * (len(dims) - dim - 1))

    loudness = one(*cuts[0])
    for cut in cuts[1:]:
        loudness = loudness * one(*cut)
    return loudness


def shared_out(key, own, number, rows, amount, top, bound, skew):
    ranking = jax.random.permutation(key, amount)
    heavy_load, usual = shares(amount, rows * top, bound, skew, True), shares(amount, rows * top, bound, skew, False)
    places = jnp.arange(amount)

    def named(lengths, offset_by):
        used = int((lengths > 0).sum())
        fixed = max(1, used // 4)
        passed = fixed + (places - fixed + offset_by * (used - fixed)) % max(1, amount - fixed)
        return jnp.zeros((amount,), jnp.int32).at[ranking[jnp.where(places < fixed, places, passed)]].set(jnp.asarray(lengths, jnp.int32))

    lengths = jnp.where(number % 4 == 0, named(heavy_load, number // 4), named(usual, number - number // 4 - 1))
    mixed = jax.random.permutation(jax.random.fold_in(own, 3), amount)
    donor, taker = mixed[0:amount // 2 * 2:2], mixed[1:amount // 2 * 2:2]
    slack = jnp.minimum(lengths[donor] - 1, bound - lengths[taker]) // 2
    slack = jnp.where((donor == ranking[0]) | (taker == ranking[0]) | (lengths[taker] == 0), 0, jnp.maximum(slack, 0))
    passed = jax.random.randint(jax.random.fold_in(own, 4), (amount // 2,), 0, 1 << 20) % (slack + 1)
    lengths = lengths.at[donor].add(-passed).at[taker].add(passed)
    items = jnp.searchsorted(jnp.cumsum(lengths), jnp.arange(rows * top), side="right").astype(jnp.int32)
    table = items.reshape(top, rows).T
    table = table[jax.random.permutation(jax.random.fold_in(own, 1), rows)]
    offset_by = jax.random.randint(jax.random.fold_in(own, 2), (rows, 1), 0, top)
    return jnp.take_along_axis(table, (jnp.arange(top)[None, :] + offset_by) % top, axis=1)


def shares(count, total, most, skew, full):
    loads = [(1 << 20) // math.isqrt(grade ** skew) + 1 for grade in range(1, count + 1)]
    largest = most if full else min(most, max(-(-total // count), total * loads[0] // sum(loads)))
    least = 1 if total - largest >= count - 1 else 0
    holding, surplus = [largest] + [least] * (count - 1), total - largest - least * (count - 1)
    while surplus > 0:
        movable = [i for i in range(1, count) if holding[i] < largest] or [i for i in range(1, count) if holding[i] < most]
        mass, remaining = sum([loads[i] for i in movable]), surplus
        for i in movable:
            addition = min(most - holding[i], max(1, remaining * loads[i] // mass), surplus)
            holding[i] = holding[i] + addition
            surplus = surplus - addition
    return np.array(holding)


def scatter_about(own_key, shape, scale, bound, cuts=(), held_as=jnp.bfloat16):
    values = scale * jax.random.normal(own_key, shape, jnp.float32)
    if cuts:
        values = values * level_of(own_key, shape, cuts, -0.22, 0.18)
    return jnp.clip(values, -bound, bound).astype(held_as)


def setup_inputs(seed: int = 0, part: int = 0) -> dict:
    key_list = jax.random.split(jax.random.key(seed), 8)
    own_keys = jax.random.split(jax.random.fold_in(key_list[7], part), 8)
    tokens = scatter_about(own_keys[0], (TOKENS, D), 1.0, 6.0, ((0, 16),))
    expert_choice_keys = jax.random.split(jax.random.fold_in(own_keys[1], 1), TOKENS // TOK_DEV)
    expert_choice_turns = jax.random.permutation(jax.random.fold_in(own_keys[1], 3), TOKENS // TOK_DEV)
    expert_choice = jax.vmap(lambda own, number: shared_out(jax.random.fold_in(own_keys[1], 2), own, number, TOK_DEV, EXPERTS, TOP, CAP, 2))(expert_choice_keys, expert_choice_turns).reshape((TOKENS, TOP))
    gate_prob = jnp.clip(jnp.exp(math.log(1.0) - 2.3025851 * jax.random.uniform(own_keys[2], (TOKENS, TOP), jnp.float32) ** level_of(own_keys[2], (TOKENS, TOP), ((0, 16),), -0.2, 0.2)), 0.1, 1.0)
    cotangent = scatter_about(own_keys[3], (TOKENS, D), 1.0, 6.0, ((0, 16),))
    w_gate = scatter_about(key_list[4], (EXPERTS, FF, D), D ** -0.5, 0.1875, ((0, 4),))
    w_up = scatter_about(key_list[5], (EXPERTS, FF, D), D ** -0.5, 0.1875, ((0, 4),))
    w_down = scatter_about(key_list[6], (EXPERTS, FF, D), FF ** -0.5, 0.21875, ((0, 4),))
    return {"tokens": tokens, "expert_choice": expert_choice, "gate_prob": gate_prob, "cotangent": cotangent, "w_gate": w_gate, "w_up": w_up, "w_down": w_down}


def contract_last(left, right):
    return lax.dot_general(left, right, (((1,), (1,)), ((), ())), preferred_element_type=jnp.float32)


def settle(value):
    return lax.optimization_barrier(value.astype(jnp.bfloat16)).astype(jnp.float32)


def group_sums(left, right):
    left_groups = left.astype(jnp.float32).reshape(N_EXPERT, N_DP, -1, left.shape[-1])
    right_groups = right.astype(jnp.float32).reshape(N_EXPERT, N_DP, -1, right.shape[-1])
    partial_sums = jnp.einsum("eqrf,eqrd->qfd", left_groups, right_groups, precision=lax.Precision.HIGHEST)
    return jnp.sum(settle(partial_sums), axis=0)


def expert_pass(operands):
    x_rows, dy_rows, gate_rows, up_rows, down_rows = operands
    part_width = FF // HID_PARTS
    out_total = jnp.zeros(x_rows.shape, jnp.float32)
    dx_total = jnp.zeros(x_rows.shape, jnp.float32)
    gate_grads, up_grads, down_grads = [], [], []
    for part_index in range(HID_PARTS):
        start = part_index * part_width
        gate_part = gate_rows[start:start + part_width]
        up_part = up_rows[start:start + part_width]
        down_part = down_rows[start:start + part_width]
        gate_pre = contract_last(x_rows, gate_part)
        up_pre = contract_last(x_rows, up_part)
        sigmoid_gate = jax.nn.sigmoid(gate_pre)
        activated = gate_pre * sigmoid_gate
        silu_slope = sigmoid_gate * (1.0 + gate_pre * (1.0 - sigmoid_gate))
        hidden = (activated * up_pre).astype(jnp.bfloat16)
        out_total = out_total + settle(jnp.dot(hidden, down_part, preferred_element_type=jnp.float32))
        d_hidden = contract_last(dy_rows, down_part)
        d_gate_pre = (d_hidden * up_pre * silu_slope).astype(jnp.bfloat16)
        d_up_pre = (d_hidden * activated).astype(jnp.bfloat16)
        dx_value = jnp.dot(d_gate_pre, gate_part, preferred_element_type=jnp.float32) + jnp.dot(d_up_pre, up_part, preferred_element_type=jnp.float32)
        dx_total = dx_total + settle(dx_value)
        gate_grads.append(group_sums(d_gate_pre, x_rows))
        up_grads.append(group_sums(d_up_pre, x_rows))
        down_grads.append(group_sums(hidden, dy_rows))
    return (out_total.astype(jnp.bfloat16), dx_total.astype(jnp.bfloat16),
            jnp.concatenate(gate_grads, axis=0).astype(jnp.bfloat16),
            jnp.concatenate(up_grads, axis=0).astype(jnp.bfloat16),
            jnp.concatenate(down_grads, axis=0).astype(jnp.bfloat16))


def reference(tokens, expert_choice, gate_prob, cotangent, w_gate, w_up, w_down):
    blocks = N_EXPERT * N_DP * N_SUB
    pair_count = TOK_DEV * TOP
    slot_total = EXPERTS * CAP
    choice_block = expert_choice.reshape(blocks, pair_count).astype(jnp.int32)
    onehot = (choice_block[:, :, None] == jnp.arange(EXPERTS, dtype=jnp.int32)[None, None, :]).astype(jnp.int32)
    before = (jnp.cumsum(onehot, axis=1) - onehot).astype(jnp.int32)
    position = jnp.sum(before * onehot, axis=2).astype(jnp.int32)
    slot_index = (choice_block * CAP + position).astype(jnp.int32)
    prob_block = gate_prob.reshape(blocks, pair_count)
    x_pairs = jnp.repeat(tokens, TOP, axis=0).reshape(blocks, pair_count, D)
    cot_pairs = jnp.repeat(cotangent, TOP, axis=0).reshape(blocks, pair_count, D)
    dy_pairs = (prob_block[:, :, None] * cot_pairs.astype(jnp.float32)).astype(jnp.bfloat16)
    block_index = jnp.arange(blocks, dtype=jnp.int32)[:, None]
    x_slots = jnp.zeros((blocks, slot_total, D), jnp.bfloat16).at[block_index, slot_index].set(x_pairs)
    dy_slots = jnp.zeros((blocks, slot_total, D), jnp.bfloat16).at[block_index, slot_index].set(dy_pairs)
    x_expert = x_slots.reshape(blocks, EXPERTS, CAP, D).transpose(1, 0, 2, 3).reshape(EXPERTS, blocks * CAP, D)
    dy_expert = dy_slots.reshape(blocks, EXPERTS, CAP, D).transpose(1, 0, 2, 3).reshape(EXPERTS, blocks * CAP, D)
    out_rows, dx_rows, grad_gate, grad_up, grad_down = lax.map(expert_pass, (x_expert, dy_expert, w_gate, w_up, w_down))
    out_slots = out_rows.reshape(EXPERTS, blocks, CAP, D).transpose(1, 0, 2, 3).reshape(blocks, slot_total, D)
    dx_slots = dx_rows.reshape(EXPERTS, blocks, CAP, D).transpose(1, 0, 2, 3).reshape(blocks, slot_total, D)
    out_pairs = out_slots[block_index, slot_index].astype(jnp.float32).reshape(TOKENS, TOP, D)
    dx_pairs = dx_slots[block_index, slot_index].astype(jnp.float32).reshape(TOKENS, TOP, D)
    layer_out = jnp.sum(gate_prob[:, :, None] * out_pairs, axis=1).astype(jnp.bfloat16)
    d_gate = jnp.sum(out_pairs * cotangent[:, None, :].astype(jnp.float32), axis=2)
    d_tokens = jnp.sum(dx_pairs, axis=1).astype(jnp.bfloat16)
    return (layer_out, d_tokens, d_gate, grad_gate, grad_up, grad_down)
```

```python
import functools

import jax
import jax.numpy as jnp
from jax import lax
from jax.experimental import pallas as pl
from jax.experimental.pallas import tpu as pltpu
from jax.sharding import PartitionSpec as P


def contract_last(left, right):
    return lax.dot_general(
        left, right, (((1,), (1,)), ((), ())), preferred_element_type=jnp.float32
    )


def contract_rows(left, right):
    return lax.dot_general(
        left, right, (((0,), (0,)), ((), ())), preferred_element_type=jnp.float32
    )


def local(tokens, expert_choice, gate_prob, cotangent, w_gate, w_up, w_down):
    n_expert = lax.axis_size("expert")
    tok_rows, feature_width = tokens.shape
    top_count = expert_choice.shape[1]
    pair_count = tok_rows * top_count
    capacity = 3 * pair_count // (2 * n_expert)
    slot_total = n_expert * capacity
    flat_choice = expert_choice.reshape(pair_count)
    onehot = (flat_choice[:, None] == jnp.arange(n_expert, dtype=jnp.int32)[None, :]).astype(
        jnp.int32
    )
    before = jnp.cumsum(onehot, axis=0) - onehot
    position = jnp.sum(before * onehot, axis=1)
    slot_index = flat_choice * capacity + position
    selector = (slot_index[None, :] == jnp.arange(slot_total, dtype=jnp.int32)[:, None]).astype(
        jnp.bfloat16
    )
    x_pairs = jnp.repeat(tokens, top_count, axis=0)
    cot_pairs = jnp.repeat(cotangent, top_count, axis=0)
    dy_pairs = (gate_prob * cot_pairs.astype(jnp.float32)).astype(jnp.bfloat16)
    x_send = jnp.dot(selector, x_pairs, preferred_element_type=jnp.float32).astype(jnp.bfloat16)
    dy_send = jnp.dot(selector, dy_pairs, preferred_element_type=jnp.float32).astype(jnp.bfloat16)
    weight_gate = w_gate[0]
    weight_up = w_up[0]
    weight_down = w_down[0]
    x_recv, dy_recv = (
        lax.all_to_all(x_send, "expert", split_axis=0, concat_axis=0, tiled=True),
        lax.all_to_all(dy_send, "expert", split_axis=0, concat_axis=0, tiled=True),
    )
    x_rows, dy_rows = (
        lax.all_gather(x_recv, "sub", axis=0, tiled=True),
        lax.all_gather(dy_recv, "sub", axis=0, tiled=True),
    )
    gate_pre = contract_last(x_rows, weight_gate)
    up_pre = contract_last(x_rows, weight_up)
    sigmoid_gate = jax.nn.sigmoid(gate_pre)
    activated = gate_pre * sigmoid_gate
    silu_slope = sigmoid_gate * (1.0 + gate_pre * (1.0 - sigmoid_gate))
    hidden = (activated * up_pre).astype(jnp.bfloat16)
    out_part = jnp.dot(hidden, weight_down, preferred_element_type=jnp.float32)
    d_hidden = contract_last(dy_rows, weight_down)
    grad_down = contract_rows(hidden, dy_rows)
    d_gate_pre = (d_hidden * up_pre * silu_slope).astype(jnp.bfloat16)
    d_up_pre = (d_hidden * activated).astype(jnp.bfloat16)
    dx_part = jnp.dot(d_gate_pre, weight_gate, preferred_element_type=jnp.float32) + jnp.dot(
        d_up_pre, weight_up, preferred_element_type=jnp.float32
    )
    grad_gate = contract_rows(d_gate_pre, x_rows)
    grad_up = contract_rows(d_up_pre, x_rows)
    summed_gate = lax.psum_scatter(
        grad_gate.astype(jnp.bfloat16), "dp", scatter_dimension=1, tiled=True
    ).astype(jnp.float32)
    summed_up = lax.psum_scatter(
        grad_up.astype(jnp.bfloat16), "dp", scatter_dimension=1, tiled=True
    ).astype(jnp.float32)
    summed_down = lax.psum_scatter(
        grad_down.astype(jnp.bfloat16), "dp", scatter_dimension=1, tiled=True
    ).astype(jnp.float32)
    out_part, dx_part, summed = (out_part, dx_part, (summed_gate, summed_up, summed_down))
    out_mine, dx_mine = (
        lax.psum_scatter(
            out_part.astype(jnp.bfloat16), "sub", scatter_dimension=0, tiled=True
        ).astype(jnp.float32),
        lax.psum_scatter(
            dx_part.astype(jnp.bfloat16), "sub", scatter_dimension=0, tiled=True
        ).astype(jnp.float32),
    )
    out_back, dx_back = (
        lax.all_to_all(
            out_mine.astype(jnp.bfloat16), "expert", split_axis=0, concat_axis=0, tiled=True
        ),
        lax.all_to_all(
            dx_mine.astype(jnp.bfloat16), "expert", split_axis=0, concat_axis=0, tiled=True
        ),
    )
    out_three = contract_rows(selector, out_back).reshape(tok_rows, top_count, feature_width)
    dx_three = contract_rows(selector, dx_back).reshape(tok_rows, top_count, feature_width)
    layer_out = jnp.sum(gate_prob[:, :, None] * out_three, axis=1).astype(jnp.bfloat16)
    d_gate = jnp.sum(out_three * cotangent[:, None, :].astype(jnp.float32), axis=2)
    d_tokens = jnp.sum(dx_three, axis=1).astype(jnp.bfloat16)
    summed_gate, summed_up, summed_down = summed
    return (
        layer_out,
        d_tokens,
        d_gate,
        summed_gate.astype(jnp.bfloat16)[None],
        summed_up.astype(jnp.bfloat16)[None],
        summed_down.astype(jnp.bfloat16)[None],
    )


LANES = 128
BLOCK = 256
MESH = pl.DeviceIdType.MESH


def matmul(left, right):
    return jnp.dot(left, right, preferred_element_type=jnp.float32)


def kernel(
    n, capacity,
    tokens_ref, choice_ref, prob_ref, cot_ref, w_gate_hbm, w_up_hbm, w_down_hbm,
    out_ref, dx_ref, d_gate_ref, grad_gate_ref, grad_up_ref, grad_down_ref,
    w_gate, w_up, w_down, x_send, y_send, x_all, y_all,
    active, slope, hidden, d_gate_pre, d_up_pre,
    active_t, slope_t, hidden_t, out_rows, dx_rows, out_back, dx_back,
    load_sem, go_sem, go_recv, fwd_sem, fwd_recv, back_sem, back_recv,
):
    me = lax.axis_index("expert")
    dp = lax.axis_index("dp")
    sibling = dp + 1 - 2 * lax.rem(dp, 2)
    across = lax.rem(dp + 2, 4)
    peers = [lax.rem(me + s, n) for s in range(n)]
    sources = [lax.rem(me + n - s, n) for s in range(n)]
    own = n * capacity
    units = w_gate.shape[0]
    features = w_gate.shape[1]
    steps = range(1, n)

    barrier = pltpu.get_barrier_semaphore()
    for s in steps:
        pl.semaphore_signal(barrier, inc=1, device_id={"expert": peers[s]}, device_id_type=MESH)
    for d in (sibling, across):
        pl.semaphore_signal(barrier, inc=1, device_id={"dp": d}, device_id_type=MESH)

    loads = [
        pltpu.make_async_copy(src, dst, load_sem.at[i])
        for i, (src, dst) in enumerate(
            ((w_gate_hbm, w_gate), (w_up_hbm, w_up), (w_down_hbm, w_down))
        )
    ]
    for load in loads:
        load.start()

    choice = choice_ref[...]
    relative = choice - me
    relative = jnp.where(relative < 0, relative + n, relative)
    tok = LANES
    row_id = lax.broadcasted_iota(jnp.int32, (tok, tok), 0)
    col_id = lax.broadcasted_iota(jnp.int32, (tok, tok), 1)
    earlier = (row_id < col_id).astype(jnp.bfloat16)
    expert_rows = max(16, n)
    onehot = lax.broadcasted_iota(jnp.int32, (expert_rows, tok), 0) == relative
    before = matmul(onehot.astype(jnp.bfloat16), earlier)
    position = jnp.sum(jnp.where(onehot, before, 0.0), axis=0, keepdims=True)
    slot = relative * capacity + position.astype(jnp.int32)
    selector = (
        lax.broadcasted_iota(jnp.int32, (own, tok), 0) == slot
    ).astype(jnp.bfloat16)
    diagonal = row_id == col_id
    prob = jnp.sum(jnp.where(diagonal, prob_ref[...], 0.0), axis=1, keepdims=True)

    def rows(s, group=0):
        return pl.ds(group * own + s * capacity, capacity)

    def dispatch(values, buffer, held, array):
        picked = matmul(selector, values).astype(jnp.bfloat16)
        held[pl.ds(0, capacity), :] = picked[:capacity]
        buffer[...] = picked[capacity:]

    def go(array, s):
        buffer, held = ((x_send, x_all), (y_send, y_all))[array]
        return pltpu.make_async_remote_copy(
            src_ref=buffer.at[pl.ds((s - 1) * capacity, capacity)],
            dst_ref=held.at[rows(s)],
            send_sem=go_sem.at[array, s],
            recv_sem=go_recv.at[array, s],
            device_id={"expert": peers[s]},
            device_id_type=MESH,
        )

    def forward(array, s, kind):
        held = (x_all, y_all)[array]
        came, lands, target = ((0, 1, sibling), (0, 2, across), (2, 3, sibling))[kind]
        return pltpu.make_async_remote_copy(
            src_ref=held.at[rows(s, came)],
            dst_ref=held.at[rows(s, lands)],
            send_sem=fwd_sem.at[array, kind, s],
            recv_sem=fwd_recv.at[array, kind, s],
            device_id={"dp": target},
            device_id_type=MESH,
        )

    def back(array, s):
        made, held = ((out_rows, out_back), (dx_rows, dx_back))[array]
        return pltpu.make_async_remote_copy(
            src_ref=made.at[rows(s)],
            dst_ref=held.at[rows(s)],
            send_sem=back_sem.at[array, s],
            recv_sem=back_recv.at[array, s],
            device_id={"expert": sources[s]},
            device_id_type=MESH,
        )

    dispatch(tokens_ref[...], x_send, x_all, 0)
    pl.semaphore_wait(barrier, n + 1)
    for s in steps:
        go(0, s).start()
    forward(0, 0, 1).start()
    forward(0, 0, 0).start()
    scaled = (prob * cot_ref[...].astype(jnp.float32)).astype(jnp.bfloat16)
    dispatch(scaled, y_send, y_all, 1)
    for s in steps:
        go(1, s).start()
    forward(1, 0, 1).start()
    forward(1, 0, 0).start()

    tail = out_back.shape[0] - own
    if tail:
        out_back[pl.ds(own, tail), :] = jnp.zeros((tail, features), jnp.bfloat16)
        dx_back[pl.ds(own, tail), :] = jnp.zeros((tail, features), jnp.bfloat16)
    for load in loads:
        load.wait()

    for s in steps:
        go(0, s).wait_recv()
        forward(0, s, 1).start()
        forward(0, s, 0).start()

    def parts_of(gate_pre, up_pre):
        sigmoid = jax.nn.sigmoid(gate_pre)
        activated = gate_pre * sigmoid
        sloped = up_pre * (sigmoid * (1.0 + gate_pre * (1.0 - sigmoid)))
        return activated, sloped, (activated * up_pre).astype(jnp.bfloat16)

    mine = pl.ds(0, own)

    def own_forward(u, carry):
        cut = pl.ds(pl.multiple_of(u * BLOCK, BLOCK), BLOCK)
        x = x_all[mine, :]
        activated, sloped, made = parts_of(
            contract_last(x, w_gate[cut, :]), contract_last(x, w_up[cut, :])
        )
        active[:, cut] = activated
        slope[:, cut] = sloped
        hidden[:, cut] = made
        return carry

    lax.fori_loop(0, units // BLOCK, own_forward, 0)

    def own_out(j, carry):
        cut = pl.ds(pl.multiple_of(j * BLOCK, BLOCK), BLOCK)
        out_rows[:, cut] = matmul(hidden[...], w_down[:, cut]).astype(jnp.bfloat16)
        return carry

    lax.fori_loop(0, features // BLOCK, own_out, 0)
    for s in steps:
        back(0, s).start()
    out_back[pl.ds(0, capacity), :] = out_rows[pl.ds(0, capacity), :]

    for s in range(n):
        forward(0, s, 1).wait_recv()
        forward(0, s, 2).start()
    for kind in (0, 2):
        for s in range(n):
            forward(0, s, kind).wait_recv()

    def all_forward(u, carry):
        cut = pl.ds(pl.multiple_of(u * BLOCK, BLOCK), BLOCK)
        x = x_all[...]
        activated, sloped, made = parts_of(
            contract_last(w_gate[cut, :], x), contract_last(w_up[cut, :], x)
        )
        active_t[cut, :] = activated
        slope_t[cut, :] = sloped
        hidden_t[cut, :] = made
        return carry

    lax.fori_loop(0, units // BLOCK, all_forward, 0)

    for s in steps:
        go(1, s).wait_recv()
        forward(1, s, 1).start()
        forward(1, s, 0).start()

    def own_backward(u, carry):
        cut = pl.ds(pl.multiple_of(u * BLOCK, BLOCK), BLOCK)
        d_hidden = contract_last(y_all[mine, :], w_down[cut, :])
        d_gate_pre[:, cut] = (d_hidden * slope[:, cut]).astype(jnp.bfloat16)
        d_up_pre[:, cut] = (d_hidden * active[:, cut]).astype(jnp.bfloat16)
        return carry

    lax.fori_loop(0, units // BLOCK, own_backward, 0)

    def own_dx(j, carry):
        cut = pl.ds(pl.multiple_of(j * BLOCK, BLOCK), BLOCK)
        dx_rows[:, cut] = (
            matmul(d_gate_pre[...], w_gate[:, cut]) + matmul(d_up_pre[...], w_up[:, cut])
        ).astype(jnp.bfloat16)
        return carry

    lax.fori_loop(0, features // BLOCK, own_dx, 0)
    for s in steps:
        back(1, s).start()
    dx_back[pl.ds(0, capacity), :] = dx_rows[pl.ds(0, capacity), :]

    for s in range(n):
        forward(1, s, 1).wait_recv()
        forward(1, s, 2).start()
    for kind in (0, 2):
        for s in range(n):
            forward(1, s, kind).wait_recv()

    width = grad_gate_ref.shape[1]
    columns = pl.ds(pl.multiple_of(dp * width, width), width)

    def all_backward(u, carry):
        cut = pl.ds(pl.multiple_of(u * BLOCK, BLOCK), BLOCK)
        d_hidden = contract_last(w_down[cut, :], y_all[...])
        left_gate = (d_hidden * slope_t[cut, :]).astype(jnp.bfloat16)
        left_up = (d_hidden * active_t[cut, :]).astype(jnp.bfloat16)
        x = x_all[:, columns]
        grad_gate_ref[cut, :] = matmul(left_gate, x).astype(jnp.bfloat16)
        grad_up_ref[cut, :] = matmul(left_up, x).astype(jnp.bfloat16)
        grad_down_ref[cut, :] = matmul(hidden_t[cut, :], y_all[:, columns]).astype(jnp.bfloat16)
        return carry

    lax.fori_loop(0, units // BLOCK, all_backward, 0)

    slot_column = jnp.sum(jnp.where(diagonal, slot, 0), axis=1, keepdims=True)
    combine = (
        lax.broadcasted_iota(jnp.int32, (tok, out_back.shape[0]), 1) == slot_column
    ).astype(jnp.bfloat16)
    for s in steps:
        back(0, s).wait_recv()
    expert_out = matmul(combine, out_back[...])
    out_ref[...] = (prob * expert_out).astype(jnp.bfloat16)
    d_gate = jnp.sum(expert_out * cot_ref[...].astype(jnp.float32), axis=1, keepdims=True)
    d_gate_ref[...] = jnp.sum(jnp.where(diagonal, d_gate, 0.0), axis=0, keepdims=True)
    for s in steps:
        back(1, s).wait_recv()
    dx_ref[...] = matmul(combine, dx_back[...]).astype(jnp.bfloat16)

    for array in range(2):
        for s in steps:
            go(array, s).wait_send()
            back(array, s).wait_send()
        for kind in range(3):
            for s in range(n):
                forward(array, s, kind).wait_send()


def fused(n, tokens, expert_choice, gate_prob, cotangent, w_gate, w_up, w_down):
    tok, features = tokens.shape
    units = w_gate.shape[1]
    capacity = 3 * tok // (2 * n)
    own = n * capacity
    everyone = 4 * own
    padded = -(-own // LANES) * LANES
    width = features // 4
    bf16, f32 = jnp.bfloat16, jnp.float32
    vmem = pl.BlockSpec(memory_space=pltpu.VMEM)
    hbm = pl.BlockSpec(memory_space=pl.ANY)
    work = 2 * units * features * (6 * own + 3 * everyone + 3 * own)
    layer_out, d_tokens, d_gate, *grads = pl.pallas_call(
        functools.partial(kernel, n, capacity),
        out_shape=(
            jax.ShapeDtypeStruct((tok, features), bf16),
            jax.ShapeDtypeStruct((tok, features), bf16),
            jax.ShapeDtypeStruct((1, tok), f32),
        )
        + (jax.ShapeDtypeStruct((units, width), bf16),) * 3,
        in_specs=[vmem] * 4 + [hbm] * 3,
        out_specs=(vmem,) * 6,
        scratch_shapes=[
            pltpu.VMEM((units, features), bf16),
            pltpu.VMEM((units, features), bf16),
            pltpu.VMEM((units, features), bf16),
            pltpu.VMEM((own - capacity, features), bf16),
            pltpu.VMEM((own - capacity, features), bf16),
            pltpu.VMEM((everyone, features), bf16),
            pltpu.VMEM((everyone, features), bf16),
            pltpu.VMEM((own, units), f32),
            pltpu.VMEM((own, units), f32),
            pltpu.VMEM((own, units), bf16),
            pltpu.VMEM((own, units), bf16),
            pltpu.VMEM((own, units), bf16),
            pltpu.VMEM((units, everyone), f32),
            pltpu.VMEM((units, everyone), f32),
            pltpu.VMEM((units, everyone), bf16),
            pltpu.VMEM((own, features), bf16),
            pltpu.VMEM((own, features), bf16),
            pltpu.VMEM((padded, features), bf16),
            pltpu.VMEM((padded, features), bf16),
            pltpu.SemaphoreType.DMA((3,)),
            pltpu.SemaphoreType.DMA((2, n)),
            pltpu.SemaphoreType.DMA((2, n)),
            pltpu.SemaphoreType.DMA((2, 3, n)),
            pltpu.SemaphoreType.DMA((2, 3, n)),
            pltpu.SemaphoreType.DMA((2, n)),
            pltpu.SemaphoreType.DMA((2, n)),
        ],
        cost_estimate=pl.CostEstimate(
            flops=work, bytes_accessed=6 * units * features, transcendentals=units * everyone
        ),
        compiler_params=pltpu.CompilerParams(
            collective_id=0, has_side_effects=True, vmem_limit_bytes=40 * 1024 * 1024
        ),
    )(
        tokens,
        expert_choice.reshape(1, tok),
        gate_prob.reshape(1, tok),
        cotangent,
        w_gate[0],
        w_up[0],
        w_down[0],
    )
    return (layer_out, d_tokens, d_gate.reshape(tok, 1), *(grad[None] for grad in grads))


def solution(mesh):
    in_specs = (
        P(("parts", "expert", "dp", "sub"), None),
        P(("parts", "expert", "dp", "sub"), None),
        P(("parts", "expert", "dp", "sub"), None),
        P(("parts", "expert", "dp", "sub"), None),
        P("expert", "sub", None),
        P("expert", "sub", None),
        P("expert", "sub", None),
    )
    out_specs = (
        P(("parts", "expert", "dp", "sub"), None),
        P(("parts", "expert", "dp", "sub"), None),
        P(("parts", "expert", "dp", "sub"), None),
        P(("parts", "expert"), "sub", "dp"),
        P(("parts", "expert"), "sub", "dp"),
        P(("parts", "expert"), "sub", "dp"),
    )
    shape = dict(mesh.shape)
    fits = shape["sub"] == 1 and shape["dp"] == 4

    def device_part(tokens, expert_choice, *rest):
        capacity = 3 * tokens.shape[0] // (2 * shape["expert"])
        one_choice = expert_choice.shape[1] == 1
        if fits and one_choice and tokens.shape[0] == LANES and capacity % 16 == 0:
            return fused(shape["expert"], tokens, expert_choice, *rest)
        return local(tokens, expert_choice, *rest)

    return jax.shard_map(device_part, mesh=mesh, in_specs=in_specs, out_specs=out_specs, check_vma=False)
```

```python
import functools

import jax
import jax.numpy as jnp
from jax import lax
from jax.experimental import pallas as pl
from jax.experimental.pallas import tpu as pltpu
from jax.sharding import PartitionSpec as P


def contract_last(left, right):
    return lax.dot_general(
        left, right, (((1,), (1,)), ((), ())), preferred_element_type=jnp.float32
    )


def contract_rows(left, right):
    return lax.dot_general(
        left, right, (((0,), (0,)), ((), ())), preferred_element_type=jnp.float32
    )


def local(tokens, expert_choice, gate_prob, cotangent, w_gate, w_up, w_down):
    n_expert = lax.axis_size("expert")
    tok_rows, feature_width = tokens.shape
    top_count = expert_choice.shape[1]
    pair_count = tok_rows * top_count
    capacity = 3 * pair_count // (2 * n_expert)
    slot_total = n_expert * capacity
    flat_choice = expert_choice.reshape(pair_count)
    onehot = (flat_choice[:, None] == jnp.arange(n_expert, dtype=jnp.int32)[None, :]).astype(
        jnp.int32
    )
    before = jnp.cumsum(onehot, axis=0) - onehot
    position = jnp.sum(before * onehot, axis=1)
    slot_index = flat_choice * capacity + position
    selector = (slot_index[None, :] == jnp.arange(slot_total, dtype=jnp.int32)[:, None]).astype(
        jnp.bfloat16
    )
    x_pairs = jnp.repeat(tokens, top_count, axis=0)
    cot_pairs = jnp.repeat(cotangent, top_count, axis=0)
    dy_pairs = (gate_prob * cot_pairs.astype(jnp.float32)).astype(jnp.bfloat16)
    x_send = jnp.dot(selector, x_pairs, preferred_element_type=jnp.float32).astype(jnp.bfloat16)
    dy_send = jnp.dot(selector, dy_pairs, preferred_element_type=jnp.float32).astype(jnp.bfloat16)
    weight_gate = w_gate[0]
    weight_up = w_up[0]
    weight_down = w_down[0]
    x_recv, dy_recv = (
        lax.all_to_all(x_send, "expert", split_axis=0, concat_axis=0, tiled=True),
        lax.all_to_all(dy_send, "expert", split_axis=0, concat_axis=0, tiled=True),
    )
    x_rows, dy_rows = (
        lax.all_gather(x_recv, "sub", axis=0, tiled=True),
        lax.all_gather(dy_recv, "sub", axis=0, tiled=True),
    )
    gate_pre = contract_last(x_rows, weight_gate)
    up_pre = contract_last(x_rows, weight_up)
    sigmoid_gate = jax.nn.sigmoid(gate_pre)
    activated = gate_pre * sigmoid_gate
    silu_slope = sigmoid_gate * (1.0 + gate_pre * (1.0 - sigmoid_gate))
    hidden = (activated * up_pre).astype(jnp.bfloat16)
    out_part = jnp.dot(hidden, weight_down, preferred_element_type=jnp.float32)
    d_hidden = contract_last(dy_rows, weight_down)
    grad_down = contract_rows(hidden, dy_rows)
    d_gate_pre = (d_hidden * up_pre * silu_slope).astype(jnp.bfloat16)
    d_up_pre = (d_hidden * activated).astype(jnp.bfloat16)
    dx_part = jnp.dot(d_gate_pre, weight_gate, preferred_element_type=jnp.float32) + jnp.dot(
        d_up_pre, weight_up, preferred_element_type=jnp.float32
    )
    grad_gate = contract_rows(d_gate_pre, x_rows)
    grad_up = contract_rows(d_up_pre, x_rows)
    summed_gate = lax.psum_scatter(
        grad_gate.astype(jnp.bfloat16), "dp", scatter_dimension=1, tiled=True
    ).astype(jnp.float32)
    summed_up = lax.psum_scatter(
        grad_up.astype(jnp.bfloat16), "dp", scatter_dimension=1, tiled=True
    ).astype(jnp.float32)
    summed_down = lax.psum_scatter(
        grad_down.astype(jnp.bfloat16), "dp", scatter_dimension=1, tiled=True
    ).astype(jnp.float32)
    out_part, dx_part, summed = (out_part, dx_part, (summed_gate, summed_up, summed_down))
    out_mine, dx_mine = (
        lax.psum_scatter(
            out_part.astype(jnp.bfloat16), "sub", scatter_dimension=0, tiled=True
        ).astype(jnp.float32),
        lax.psum_scatter(
            dx_part.astype(jnp.bfloat16), "sub", scatter_dimension=0, tiled=True
        ).astype(jnp.float32),
    )
    out_back, dx_back = (
        lax.all_to_all(
            out_mine.astype(jnp.bfloat16), "expert", split_axis=0, concat_axis=0, tiled=True
        ),
        lax.all_to_all(
            dx_mine.astype(jnp.bfloat16), "expert", split_axis=0, concat_axis=0, tiled=True
        ),
    )
    out_three = contract_rows(selector, out_back).reshape(tok_rows, top_count, feature_width)
    dx_three = contract_rows(selector, dx_back).reshape(tok_rows, top_count, feature_width)
    layer_out = jnp.sum(gate_prob[:, :, None] * out_three, axis=1).astype(jnp.bfloat16)
    d_gate = jnp.sum(out_three * cotangent[:, None, :].astype(jnp.float32), axis=2)
    d_tokens = jnp.sum(dx_three, axis=1).astype(jnp.bfloat16)
    summed_gate, summed_up, summed_down = summed
    return (
        layer_out,
        d_tokens,
        d_gate,
        summed_gate.astype(jnp.bfloat16)[None],
        summed_up.astype(jnp.bfloat16)[None],
        summed_down.astype(jnp.bfloat16)[None],
    )


LANES = 128
BLOCK = 256
MESH = pl.DeviceIdType.MESH


def matmul(left, right):
    return jnp.dot(left, right, preferred_element_type=jnp.float32)


def kernel(
    n, capacity,
    tokens_hbm, choice_hbm, prob_hbm, cot_hbm, w_gate_hbm, w_up_hbm, w_down_hbm,
    out_hbm, dx_hbm, d_gate_hbm, grad_gate_hbm, grad_up_hbm, grad_down_hbm,
    tokens_ref, choice_ref, prob_ref, cot_ref,
    w_gate, w_up, w_down, x_send, y_send, x_all, y_all,
    active, slope, hidden, d_gate_pre, d_up_pre,
    active_t, slope_t, hidden_t, out_rows, dx_rows, out_back, dx_back,
    out_ref, dx_ref, d_gate_ref, grad_gate_ref, grad_up_ref, grad_down_ref,
    load_sem, store_sem, go_sem, go_recv, fwd_sem, fwd_recv, back_sem, back_recv,
):
    loads = [
        pltpu.make_async_copy(src, dst, load_sem.at[i])
        for i, (src, dst) in enumerate(
            (
                (choice_hbm, choice_ref),
                (tokens_hbm, tokens_ref),
                (prob_hbm, prob_ref),
                (cot_hbm, cot_ref),
                (w_gate_hbm, w_gate),
                (w_up_hbm, w_up),
                (w_down_hbm, w_down),
            )
        )
    ]
    for load in loads:
        load.start()
    stores = [
        pltpu.make_async_copy(src, dst, store_sem.at[i])
        for i, (src, dst) in enumerate(
            (
                (out_ref, out_hbm),
                (dx_ref, dx_hbm),
                (d_gate_ref, d_gate_hbm),
                (grad_gate_ref, grad_gate_hbm),
                (grad_up_ref, grad_up_hbm),
                (grad_down_ref, grad_down_hbm),
            )
        )
    ]
    me = lax.axis_index("expert")
    dp = lax.axis_index("dp")
    sibling = dp + 1 - 2 * lax.rem(dp, 2)
    across = lax.rem(dp + 2, 4)
    peers = [lax.rem(me + s, n) for s in range(n)]
    sources = [lax.rem(me + n - s, n) for s in range(n)]
    own = n * capacity
    units = w_gate.shape[0]
    features = w_gate.shape[1]
    steps = range(1, n)

    barrier = pltpu.get_barrier_semaphore()
    for s in steps:
        pl.semaphore_signal(barrier, inc=1, device_id={"expert": peers[s]}, device_id_type=MESH)
    for d in (sibling, across):
        pl.semaphore_signal(barrier, inc=1, device_id={"dp": d}, device_id_type=MESH)

    loads[0].wait()
    choice = choice_ref[...]
    relative = choice - me
    relative = jnp.where(relative < 0, relative + n, relative)
    tok = LANES
    row_id = lax.broadcasted_iota(jnp.int32, (tok, tok), 0)
    col_id = lax.broadcasted_iota(jnp.int32, (tok, tok), 1)
    earlier = (row_id < col_id).astype(jnp.bfloat16)
    expert_rows = max(16, n)
    onehot = lax.broadcasted_iota(jnp.int32, (expert_rows, tok), 0) == relative
    before = matmul(onehot.astype(jnp.bfloat16), earlier)
    position = jnp.sum(jnp.where(onehot, before, 0.0), axis=0, keepdims=True)
    slot = relative * capacity + position.astype(jnp.int32)
    selector = (
        lax.broadcasted_iota(jnp.int32, (own, tok), 0) == slot
    ).astype(jnp.bfloat16)
    diagonal = row_id == col_id

    def rows(s, group=0):
        return pl.ds(group * own + s * capacity, capacity)

    def dispatch(values, buffer, held, array):
        picked = matmul(selector, values).astype(jnp.bfloat16)
        held[pl.ds(0, capacity), :] = picked[:capacity]
        buffer[...] = picked[capacity:]

    def go(array, s):
        buffer, held = ((x_send, x_all), (y_send, y_all))[array]
        return pltpu.make_async_remote_copy(
            src_ref=buffer.at[pl.ds((s - 1) * capacity, capacity)],
            dst_ref=held.at[rows(s)],
            send_sem=go_sem.at[array, s],
            recv_sem=go_recv.at[array, s],
            device_id={"expert": peers[s]},
            device_id_type=MESH,
        )

    def forward(array, s, kind):
        held = (x_all, y_all)[array]
        came, lands, target = ((0, 1, sibling), (0, 2, across), (2, 3, sibling))[kind]
        return pltpu.make_async_remote_copy(
            src_ref=held.at[rows(s, came)],
            dst_ref=held.at[rows(s, lands)],
            send_sem=fwd_sem.at[array, kind, s],
            recv_sem=fwd_recv.at[array, kind, s],
            device_id={"dp": target},
            device_id_type=MESH,
        )

    def back(array, s):
        made, held = ((out_rows, out_back), (dx_rows, dx_back))[array]
        return pltpu.make_async_remote_copy(
            src_ref=made.at[rows(s)],
            dst_ref=held.at[rows(s)],
            send_sem=back_sem.at[array, s],
            recv_sem=back_recv.at[array, s],
            device_id={"expert": sources[s]},
            device_id_type=MESH,
        )

    loads[1].wait()
    dispatch(tokens_ref[...], x_send, x_all, 0)
    pl.semaphore_wait(barrier, n + 1)
    for s in steps:
        go(0, s).start()
    forward(0, 0, 1).start()
    forward(0, 0, 0).start()
    loads[2].wait()
    loads[3].wait()
    prob = jnp.sum(jnp.where(diagonal, prob_ref[...], 0.0), axis=1, keepdims=True)
    scaled = (prob * cot_ref[...].astype(jnp.float32)).astype(jnp.bfloat16)
    dispatch(scaled, y_send, y_all, 1)
    for s in steps:
        go(1, s).start()
    forward(1, 0, 1).start()
    forward(1, 0, 0).start()

    tail = out_back.shape[0] - own
    if tail:
        out_back[pl.ds(own, tail), :] = jnp.zeros((tail, features), jnp.bfloat16)
        dx_back[pl.ds(own, tail), :] = jnp.zeros((tail, features), jnp.bfloat16)
    for load in loads[4:]:
        load.wait()

    for s in steps:
        go(0, s).wait_recv()
        forward(0, s, 1).start()
        forward(0, s, 0).start()

    def parts_of(gate_pre, up_pre):
        sigmoid = jax.nn.sigmoid(gate_pre)
        activated = gate_pre * sigmoid
        sloped = up_pre * (sigmoid * (1.0 + gate_pre * (1.0 - sigmoid)))
        return activated, sloped, (activated * up_pre).astype(jnp.bfloat16)

    mine = pl.ds(0, own)

    def own_forward(u, carry):
        cut = pl.ds(pl.multiple_of(u * BLOCK, BLOCK), BLOCK)
        x = x_all[mine, :]
        activated, sloped, made = parts_of(
            contract_last(x, w_gate[cut, :]), contract_last(x, w_up[cut, :])
        )
        active[:, cut] = activated
        slope[:, cut] = sloped
        hidden[:, cut] = made
        return carry

    lax.fori_loop(0, units // BLOCK, own_forward, 0)

    def own_out(j, carry):
        cut = pl.ds(pl.multiple_of(j * BLOCK, BLOCK), BLOCK)
        out_rows[:, cut] = matmul(hidden[...], w_down[:, cut]).astype(jnp.bfloat16)
        return carry

    lax.fori_loop(0, features // BLOCK, own_out, 0)
    for s in steps:
        back(0, s).start()
    out_back[pl.ds(0, capacity), :] = out_rows[pl.ds(0, capacity), :]

    for s in range(n):
        forward(0, s, 1).wait_recv()
        forward(0, s, 2).start()
    for kind in (0, 2):
        for s in range(n):
            forward(0, s, kind).wait_recv()

    def all_forward(u, carry):
        cut = pl.ds(pl.multiple_of(u * BLOCK, BLOCK), BLOCK)
        x = x_all[...]
        activated, sloped, made = parts_of(
            contract_last(w_gate[cut, :], x), contract_last(w_up[cut, :], x)
        )
        active_t[cut, :] = activated
        slope_t[cut, :] = sloped
        hidden_t[cut, :] = made
        return carry

    lax.fori_loop(0, units // BLOCK, all_forward, 0)

    for s in steps:
        go(1, s).wait_recv()
        forward(1, s, 1).start()
        forward(1, s, 0).start()

    def own_backward(u, carry):
        cut = pl.ds(pl.multiple_of(u * BLOCK, BLOCK), BLOCK)
        d_hidden = contract_last(y_all[mine, :], w_down[cut, :])
        d_gate_pre[:, cut] = (d_hidden * slope[:, cut]).astype(jnp.bfloat16)
        d_up_pre[:, cut] = (d_hidden * active[:, cut]).astype(jnp.bfloat16)
        return carry

    lax.fori_loop(0, units // BLOCK, own_backward, 0)

    def own_dx(j, carry):
        cut = pl.ds(pl.multiple_of(j * BLOCK, BLOCK), BLOCK)
        dx_rows[:, cut] = (
            matmul(d_gate_pre[...], w_gate[:, cut]) + matmul(d_up_pre[...], w_up[:, cut])
        ).astype(jnp.bfloat16)
        return carry

    lax.fori_loop(0, features // BLOCK, own_dx, 0)
    for s in steps:
        back(1, s).start()
    dx_back[pl.ds(0, capacity), :] = dx_rows[pl.ds(0, capacity), :]

    for s in range(n):
        forward(1, s, 1).wait_recv()
        forward(1, s, 2).start()
    for kind in (0, 2):
        for s in range(n):
            forward(1, s, kind).wait_recv()

    width = grad_gate_ref.shape[1]
    columns = pl.ds(pl.multiple_of(dp * width, width), width)

    def all_backward(u, carry):
        cut = pl.ds(pl.multiple_of(u * BLOCK, BLOCK), BLOCK)
        d_hidden = contract_last(w_down[cut, :], y_all[...])
        left_gate = (d_hidden * slope_t[cut, :]).astype(jnp.bfloat16)
        left_up = (d_hidden * active_t[cut, :]).astype(jnp.bfloat16)
        x = x_all[:, columns]
        grad_gate_ref[cut, :] = matmul(left_gate, x).astype(jnp.bfloat16)
        grad_up_ref[cut, :] = matmul(left_up, x).astype(jnp.bfloat16)
        grad_down_ref[cut, :] = matmul(hidden_t[cut, :], y_all[:, columns]).astype(jnp.bfloat16)
        return carry

    lax.fori_loop(0, units // BLOCK, all_backward, 0)

    for store in stores[3:]:
        store.start()
    slot_column = jnp.sum(jnp.where(diagonal, slot, 0), axis=1, keepdims=True)
    combine = (
        lax.broadcasted_iota(jnp.int32, (tok, out_back.shape[0]), 1) == slot_column
    ).astype(jnp.bfloat16)
    for s in steps:
        back(0, s).wait_recv()
    expert_out = matmul(combine, out_back[...])
    out_ref[...] = (prob * expert_out).astype(jnp.bfloat16)
    d_gate = jnp.sum(expert_out * cot_ref[...].astype(jnp.float32), axis=1, keepdims=True)
    d_gate_ref[...] = jnp.sum(jnp.where(diagonal, d_gate, 0.0), axis=0, keepdims=True)
    stores[0].start()
    stores[2].start()
    for s in steps:
        back(1, s).wait_recv()
    dx_ref[...] = matmul(combine, dx_back[...]).astype(jnp.bfloat16)
    stores[1].start()

    for array in range(2):
        for s in steps:
            go(array, s).wait_send()
            back(array, s).wait_send()
        for kind in range(3):
            for s in range(n):
                forward(array, s, kind).wait_send()
    for store in stores:
        store.wait()


def write_out(*refs):
    made, results, sem = refs[:6], refs[6:12], refs[12]
    copies = [
        pltpu.make_async_copy(src, dst, sem.at[i])
        for i, (src, dst) in enumerate(zip(made, results))
    ]
    for copy in copies:
        copy.start()
    for copy in copies:
        copy.wait()


def fused(n, tokens, expert_choice, gate_prob, cotangent, w_gate, w_up, w_down):
    tok, features = tokens.shape
    units = w_gate.shape[1]
    capacity = 3 * tok // (2 * n)
    own = n * capacity
    everyone = 4 * own
    padded = -(-own // LANES) * LANES
    width = features // 4
    bf16, f32 = jnp.bfloat16, jnp.float32
    hbm = pl.BlockSpec(memory_space=pltpu.HBM)
    work = 2 * units * features * (6 * own + 3 * everyone + 3 * own)
    results = pl.pallas_call(
        functools.partial(kernel, n, capacity),
        out_shape=(
            jax.ShapeDtypeStruct((tok, features), bf16),
            jax.ShapeDtypeStruct((tok, features), bf16),
            jax.ShapeDtypeStruct((1, tok), f32),
        )
        + (jax.ShapeDtypeStruct((units, width), bf16),) * 3,
        in_specs=[hbm] * 7,
        out_specs=(hbm,) * 6,
        scratch_shapes=[
            pltpu.VMEM((tok, features), bf16),
            pltpu.VMEM((1, tok), jnp.int32),
            pltpu.VMEM((1, tok), f32),
            pltpu.VMEM((tok, features), bf16),
            pltpu.VMEM((units, features), bf16),
            pltpu.VMEM((units, features), bf16),
            pltpu.VMEM((units, features), bf16),
            pltpu.VMEM((own - capacity, features), bf16),
            pltpu.VMEM((own - capacity, features), bf16),
            pltpu.VMEM((everyone, features), bf16),
            pltpu.VMEM((everyone, features), bf16),
            pltpu.VMEM((own, units), f32),
            pltpu.VMEM((own, units), f32),
            pltpu.VMEM((own, units), bf16),
            pltpu.VMEM((own, units), bf16),
            pltpu.VMEM((own, units), bf16),
            pltpu.VMEM((units, everyone), f32),
            pltpu.VMEM((units, everyone), f32),
            pltpu.VMEM((units, everyone), bf16),
            pltpu.VMEM((own, features), bf16),
            pltpu.VMEM((own, features), bf16),
            pltpu.VMEM((padded, features), bf16),
            pltpu.VMEM((padded, features), bf16),
            pltpu.VMEM((tok, features), bf16),
            pltpu.VMEM((tok, features), bf16),
            pltpu.VMEM((1, tok), f32),
            pltpu.VMEM((units, width), bf16),
            pltpu.VMEM((units, width), bf16),
            pltpu.VMEM((units, width), bf16),
            pltpu.SemaphoreType.DMA((7,)),
            pltpu.SemaphoreType.DMA((6,)),
            pltpu.SemaphoreType.DMA((2, n)),
            pltpu.SemaphoreType.DMA((2, n)),
            pltpu.SemaphoreType.DMA((2, 3, n)),
            pltpu.SemaphoreType.DMA((2, 3, n)),
            pltpu.SemaphoreType.DMA((2, n)),
            pltpu.SemaphoreType.DMA((2, n)),
        ],
        cost_estimate=pl.CostEstimate(
            flops=work, bytes_accessed=6 * units * features, transcendentals=units * everyone
        ),
        compiler_params=pltpu.CompilerParams(
            collective_id=0, has_side_effects=True, vmem_limit_bytes=60 * 1024 * 1024
        ),
    )(
        tokens,
        expert_choice.reshape(1, tok),
        gate_prob.reshape(1, tok),
        cotangent,
        w_gate[0],
        w_up[0],
        w_down[0],
    )
    layer_out, d_tokens, d_gate, *grads = pl.pallas_call(
        write_out,
        out_shape=tuple(jax.ShapeDtypeStruct(r.shape, r.dtype) for r in results),
        in_specs=[hbm] * 6,
        out_specs=(hbm,) * 6,
        scratch_shapes=[pltpu.SemaphoreType.DMA((6,))],
        compiler_params=pltpu.CompilerParams(vmem_limit_bytes=60 * 1024 * 1024),
    )(*results)
    return (layer_out, d_tokens, d_gate.reshape(tok, 1), *(grad[None] for grad in grads))


def solution(mesh):
    in_specs = (
        P(("parts", "expert", "dp", "sub"), None),
        P(("parts", "expert", "dp", "sub"), None),
        P(("parts", "expert", "dp", "sub"), None),
        P(("parts", "expert", "dp", "sub"), None),
        P("expert", "sub", None),
        P("expert", "sub", None),
        P("expert", "sub", None),
    )
    out_specs = (
        P(("parts", "expert", "dp", "sub"), None),
        P(("parts", "expert", "dp", "sub"), None),
        P(("parts", "expert", "dp", "sub"), None),
        P(("parts", "expert"), "sub", "dp"),
        P(("parts", "expert"), "sub", "dp"),
        P(("parts", "expert"), "sub", "dp"),
    )
    shape = dict(mesh.shape)
    fits = shape["sub"] == 1 and shape["dp"] == 4

    def device_part(tokens, expert_choice, *rest):
        capacity = 3 * tokens.shape[0] // (2 * shape["expert"])
        one_choice = expert_choice.shape[1] == 1
        if fits and one_choice and tokens.shape[0] == LANES and capacity % 16 == 0:
            return fused(shape["expert"], tokens, expert_choice, *rest)
        return local(tokens, expert_choice, *rest)

    return jax.shard_map(device_part, mesh=mesh, in_specs=in_specs, out_specs=out_specs, check_vma=False)
```

```python
import functools

import jax
import jax.numpy as jnp
from jax import lax
from jax.experimental import pallas as pl
from jax.experimental.pallas import tpu as pltpu
from jax.sharding import PartitionSpec as P


def contract_last(left, right):
    return lax.dot_general(
        left, right, (((1,), (1,)), ((), ())), preferred_element_type=jnp.float32
    )


def contract_rows(left, right):
    return lax.dot_general(
        left, right, (((0,), (0,)), ((), ())), preferred_element_type=jnp.float32
    )


def local(tokens, expert_choice, gate_prob, cotangent, w_gate, w_up, w_down):
    n_expert = lax.axis_size("expert")
    tok_rows, feature_width = tokens.shape
    top_count = expert_choice.shape[1]
    pair_count = tok_rows * top_count
    capacity = 3 * pair_count // (2 * n_expert)
    slot_total = n_expert * capacity
    flat_choice = expert_choice.reshape(pair_count)
    onehot = (flat_choice[:, None] == jnp.arange(n_expert, dtype=jnp.int32)[None, :]).astype(
        jnp.int32
    )
    before = jnp.cumsum(onehot, axis=0) - onehot
    position = jnp.sum(before * onehot, axis=1)
    slot_index = flat_choice * capacity + position
    selector = (slot_index[None, :] == jnp.arange(slot_total, dtype=jnp.int32)[:, None]).astype(
        jnp.bfloat16
    )
    x_pairs = jnp.repeat(tokens, top_count, axis=0)
    cot_pairs = jnp.repeat(cotangent, top_count, axis=0)
    dy_pairs = (gate_prob * cot_pairs.astype(jnp.float32)).astype(jnp.bfloat16)
    x_send = jnp.dot(selector, x_pairs, preferred_element_type=jnp.float32).astype(jnp.bfloat16)
    dy_send = jnp.dot(selector, dy_pairs, preferred_element_type=jnp.float32).astype(jnp.bfloat16)
    weight_gate = w_gate[0]
    weight_up = w_up[0]
    weight_down = w_down[0]
    x_recv, dy_recv = (
        lax.all_to_all(x_send, "expert", split_axis=0, concat_axis=0, tiled=True),
        lax.all_to_all(dy_send, "expert", split_axis=0, concat_axis=0, tiled=True),
    )
    x_rows, dy_rows = (
        lax.all_gather(x_recv, "sub", axis=0, tiled=True),
        lax.all_gather(dy_recv, "sub", axis=0, tiled=True),
    )
    gate_pre = contract_last(x_rows, weight_gate)
    up_pre = contract_last(x_rows, weight_up)
    sigmoid_gate = jax.nn.sigmoid(gate_pre)
    activated = gate_pre * sigmoid_gate
    silu_slope = sigmoid_gate * (1.0 + gate_pre * (1.0 - sigmoid_gate))
    hidden = (activated * up_pre).astype(jnp.bfloat16)
    out_part = jnp.dot(hidden, weight_down, preferred_element_type=jnp.float32)
    d_hidden = contract_last(dy_rows, weight_down)
    grad_down = contract_rows(hidden, dy_rows)
    d_gate_pre = (d_hidden * up_pre * silu_slope).astype(jnp.bfloat16)
    d_up_pre = (d_hidden * activated).astype(jnp.bfloat16)
    dx_part = jnp.dot(d_gate_pre, weight_gate, preferred_element_type=jnp.float32) + jnp.dot(
        d_up_pre, weight_up, preferred_element_type=jnp.float32
    )
    grad_gate = contract_rows(d_gate_pre, x_rows)
    grad_up = contract_rows(d_up_pre, x_rows)
    summed_gate = lax.psum_scatter(
        grad_gate.astype(jnp.bfloat16), "dp", scatter_dimension=1, tiled=True
    ).astype(jnp.float32)
    summed_up = lax.psum_scatter(
        grad_up.astype(jnp.bfloat16), "dp", scatter_dimension=1, tiled=True
    ).astype(jnp.float32)
    summed_down = lax.psum_scatter(
        grad_down.astype(jnp.bfloat16), "dp", scatter_dimension=1, tiled=True
    ).astype(jnp.float32)
    out_part, dx_part, summed = (out_part, dx_part, (summed_gate, summed_up, summed_down))
    out_mine, dx_mine = (
        lax.psum_scatter(
            out_part.astype(jnp.bfloat16), "sub", scatter_dimension=0, tiled=True
        ).astype(jnp.float32),
        lax.psum_scatter(
            dx_part.astype(jnp.bfloat16), "sub", scatter_dimension=0, tiled=True
        ).astype(jnp.float32),
    )
    out_back, dx_back = (
        lax.all_to_all(
            out_mine.astype(jnp.bfloat16), "expert", split_axis=0, concat_axis=0, tiled=True
        ),
        lax.all_to_all(
            dx_mine.astype(jnp.bfloat16), "expert", split_axis=0, concat_axis=0, tiled=True
        ),
    )
    out_three = contract_rows(selector, out_back).reshape(tok_rows, top_count, feature_width)
    dx_three = contract_rows(selector, dx_back).reshape(tok_rows, top_count, feature_width)
    layer_out = jnp.sum(gate_prob[:, :, None] * out_three, axis=1).astype(jnp.bfloat16)
    d_gate = jnp.sum(out_three * cotangent[:, None, :].astype(jnp.float32), axis=2)
    d_tokens = jnp.sum(dx_three, axis=1).astype(jnp.bfloat16)
    summed_gate, summed_up, summed_down = summed
    return (
        layer_out,
        d_tokens,
        d_gate,
        summed_gate.astype(jnp.bfloat16)[None],
        summed_up.astype(jnp.bfloat16)[None],
        summed_down.astype(jnp.bfloat16)[None],
    )


LANES = 128
BLOCK = 256
MESH = pl.DeviceIdType.MESH


def matmul(left, right):
    return jnp.dot(left, right, preferred_element_type=jnp.float32)


def kernel(
    n, capacity,
    tokens_hbm, choice_hbm, prob_hbm, cot_hbm, w_gate_hbm, w_up_hbm, w_down_hbm,
    out_hbm, dx_hbm, d_gate_hbm, grad_gate_hbm, grad_up_hbm, grad_down_hbm,
    tokens_ref, choice_ref, prob_ref, cot_ref,
    w_gate, w_up, w_down, x_send, y_send, x_all, y_all,
    active, slope, hidden, d_gate_pre, d_up_pre,
    active_t, slope_t, hidden_t, out_rows, dx_rows, out_back, dx_back,
    out_ref, dx_ref, d_gate_ref, grad_gate_ref, grad_up_ref, grad_down_ref,
    load_sem, store_sem, go_sem, go_recv, fwd_sem, fwd_recv, back_sem, back_recv,
):
    loads = [
        pltpu.make_async_copy(src, dst, load_sem.at[i])
        for i, (src, dst) in enumerate(
            (
                (choice_hbm, choice_ref),
                (tokens_hbm, tokens_ref),
                (prob_hbm, prob_ref),
                (cot_hbm, cot_ref),
                (w_gate_hbm, w_gate),
                (w_up_hbm, w_up),
                (w_down_hbm, w_down),
            )
        )
    ]
    for load in loads:
        load.start()
    stores = [
        pltpu.make_async_copy(src, dst, store_sem.at[i])
        for i, (src, dst) in enumerate(
            (
                (out_ref, out_hbm),
                (dx_ref, dx_hbm),
                (d_gate_ref, d_gate_hbm),
                (grad_gate_ref, grad_gate_hbm),
                (grad_up_ref, grad_up_hbm),
                (grad_down_ref, grad_down_hbm),
            )
        )
    ]
    me = lax.axis_index("expert")
    dp = lax.axis_index("dp")
    sibling = dp + 1 - 2 * lax.rem(dp, 2)
    across = lax.rem(dp + 2, 4)
    peers = [lax.rem(me + s, n) for s in range(n)]
    sources = [lax.rem(me + n - s, n) for s in range(n)]
    own = n * capacity
    units = w_gate.shape[0]
    features = w_gate.shape[1]
    steps = range(1, n)

    barrier = pltpu.get_barrier_semaphore()
    for s in steps:
        pl.semaphore_signal(barrier, inc=1, device_id={"expert": peers[s]}, device_id_type=MESH)
    for d in (sibling, across):
        pl.semaphore_signal(barrier, inc=1, device_id={"dp": d}, device_id_type=MESH)

    loads[0].wait()
    choice = choice_ref[...]
    relative = choice - me
    relative = jnp.where(relative < 0, relative + n, relative)
    tok = LANES
    row_id = lax.broadcasted_iota(jnp.int32, (tok, tok), 0)
    col_id = lax.broadcasted_iota(jnp.int32, (tok, tok), 1)
    earlier = (row_id < col_id).astype(jnp.bfloat16)
    expert_rows = max(16, n)
    onehot = lax.broadcasted_iota(jnp.int32, (expert_rows, tok), 0) == relative
    before = matmul(onehot.astype(jnp.bfloat16), earlier)
    position = jnp.sum(jnp.where(onehot, before, 0.0), axis=0, keepdims=True)
    slot = relative * capacity + position.astype(jnp.int32)
    selector = (
        lax.broadcasted_iota(jnp.int32, (own, tok), 0) == slot
    ).astype(jnp.bfloat16)
    diagonal = row_id == col_id

    def rows(s, group=0):
        return pl.ds(group * own + s * capacity, capacity)

    def dispatch(values, buffer, held, array):
        picked = matmul(selector, values).astype(jnp.bfloat16)
        held[pl.ds(0, capacity), :] = picked[:capacity]
        buffer[...] = picked[capacity:]

    def go(array, s):
        buffer, held = ((x_send, x_all), (y_send, y_all))[array]
        return pltpu.make_async_remote_copy(
            src_ref=buffer.at[pl.ds((s - 1) * capacity, capacity)],
            dst_ref=held.at[rows(s)],
            send_sem=go_sem.at[array, s],
            recv_sem=go_recv.at[array, s],
            device_id={"expert": peers[s]},
            device_id_type=MESH,
        )

    def forward(array, s, kind):
        held = (x_all, y_all)[array]
        came, lands, target = ((0, 1, sibling), (0, 2, across), (2, 3, sibling))[kind]
        return pltpu.make_async_remote_copy(
            src_ref=held.at[rows(s, came)],
            dst_ref=held.at[rows(s, lands)],
            send_sem=fwd_sem.at[array, kind, s],
            recv_sem=fwd_recv.at[array, kind, s],
            device_id={"dp": target},
            device_id_type=MESH,
        )

    def back(array, s):
        made, held = ((out_rows, out_back), (dx_rows, dx_back))[array]
        return pltpu.make_async_remote_copy(
            src_ref=made.at[rows(s)],
            dst_ref=held.at[rows(s)],
            send_sem=back_sem.at[array, s],
            recv_sem=back_recv.at[array, s],
            device_id={"expert": sources[s]},
            device_id_type=MESH,
        )

    loads[1].wait()
    dispatch(tokens_ref[...], x_send, x_all, 0)
    pl.semaphore_wait(barrier, n + 1)
    for s in steps:
        go(0, s).start()
    forward(0, 0, 1).start()
    forward(0, 0, 0).start()
    loads[2].wait()
    loads[3].wait()
    prob = jnp.sum(jnp.where(diagonal, prob_ref[...], 0.0), axis=1, keepdims=True)
    scaled = (prob * cot_ref[...].astype(jnp.float32)).astype(jnp.bfloat16)
    dispatch(scaled, y_send, y_all, 1)
    for s in steps:
        go(1, s).start()
    forward(1, 0, 1).start()
    forward(1, 0, 0).start()

    tail = out_back.shape[0] - own
    if tail:
        out_back[pl.ds(own, tail), :] = jnp.zeros((tail, features), jnp.bfloat16)
        dx_back[pl.ds(own, tail), :] = jnp.zeros((tail, features), jnp.bfloat16)
    for load in loads[4:]:
        load.wait()

    for s in steps:
        go(0, s).wait_recv()
        forward(0, s, 1).start()
        forward(0, s, 0).start()

    def parts_of(gate_pre, up_pre):
        sigmoid = jax.nn.sigmoid(gate_pre)
        activated = gate_pre * sigmoid
        sloped = up_pre * (sigmoid * (1.0 + gate_pre * (1.0 - sigmoid)))
        return activated, sloped, (activated * up_pre).astype(jnp.bfloat16)

    mine = pl.ds(0, own)

    def own_forward(u, carry):
        cut = pl.ds(pl.multiple_of(u * BLOCK, BLOCK), BLOCK)
        x = x_all[mine, :]
        activated, sloped, made = parts_of(
            contract_last(x, w_gate[cut, :]), contract_last(x, w_up[cut, :])
        )
        active[:, cut] = activated
        slope[:, cut] = sloped
        hidden[:, cut] = made
        return carry

    lax.fori_loop(0, units // BLOCK, own_forward, 0)

    def own_out(j, carry):
        cut = pl.ds(pl.multiple_of(j * BLOCK, BLOCK), BLOCK)
        out_rows[:, cut] = matmul(hidden[...], w_down[:, cut]).astype(jnp.bfloat16)
        return carry

    lax.fori_loop(0, features // BLOCK, own_out, 0)
    for s in steps:
        back(0, s).start()
    out_back[pl.ds(0, capacity), :] = out_rows[pl.ds(0, capacity), :]

    for s in range(n):
        forward(0, s, 1).wait_recv()
        forward(0, s, 2).start()
    for kind in (0, 2):
        for s in range(n):
            forward(0, s, kind).wait_recv()

    def all_forward(u, carry):
        cut = pl.ds(pl.multiple_of(u * BLOCK, BLOCK), BLOCK)
        x = x_all[...]
        activated, sloped, made = parts_of(
            contract_last(w_gate[cut, :], x), contract_last(w_up[cut, :], x)
        )
        active_t[cut, :] = activated
        slope_t[cut, :] = sloped
        hidden_t[cut, :] = made
        return carry

    lax.fori_loop(0, units // BLOCK, all_forward, 0)

    for s in steps:
        go(1, s).wait_recv()
        forward(1, s, 1).start()
        forward(1, s, 0).start()

    def own_backward(u, carry):
        cut = pl.ds(pl.multiple_of(u * BLOCK, BLOCK), BLOCK)
        d_hidden = contract_last(y_all[mine, :], w_down[cut, :])
        d_gate_pre[:, cut] = (d_hidden * slope[:, cut]).astype(jnp.bfloat16)
        d_up_pre[:, cut] = (d_hidden * active[:, cut]).astype(jnp.bfloat16)
        return carry

    lax.fori_loop(0, units // BLOCK, own_backward, 0)

    def own_dx(j, carry):
        cut = pl.ds(pl.multiple_of(j * BLOCK, BLOCK), BLOCK)
        dx_rows[:, cut] = (
            matmul(d_gate_pre[...], w_gate[:, cut]) + matmul(d_up_pre[...], w_up[:, cut])
        ).astype(jnp.bfloat16)
        return carry

    lax.fori_loop(0, features // BLOCK, own_dx, 0)
    for s in steps:
        back(1, s).start()
    dx_back[pl.ds(0, capacity), :] = dx_rows[pl.ds(0, capacity), :]

    for s in range(n):
        forward(1, s, 1).wait_recv()
        forward(1, s, 2).start()
    for kind in (0, 2):
        for s in range(n):
            forward(1, s, kind).wait_recv()

    width = grad_gate_ref.shape[1]
    columns = pl.ds(pl.multiple_of(dp * width, width), width)

    def all_backward(u, carry):
        cut = pl.ds(pl.multiple_of(u * BLOCK, BLOCK), BLOCK)
        d_hidden = contract_last(w_down[cut, :], y_all[...])
        left_gate = (d_hidden * slope_t[cut, :]).astype(jnp.bfloat16)
        left_up = (d_hidden * active_t[cut, :]).astype(jnp.bfloat16)
        x = x_all[:, columns]
        grad_gate_ref[cut, :] = matmul(left_gate, x).astype(jnp.bfloat16)
        grad_up_ref[cut, :] = matmul(left_up, x).astype(jnp.bfloat16)
        grad_down_ref[cut, :] = matmul(hidden_t[cut, :], y_all[:, columns]).astype(jnp.bfloat16)
        return carry

    lax.fori_loop(0, units // BLOCK, all_backward, 0)

    for store in stores[3:]:
        store.start()
    slot_column = jnp.sum(jnp.where(diagonal, slot, 0), axis=1, keepdims=True)
    combine = (
        lax.broadcasted_iota(jnp.int32, (tok, out_back.shape[0]), 1) == slot_column
    ).astype(jnp.bfloat16)
    for s in steps:
        back(0, s).wait_recv()
    expert_out = matmul(combine, out_back[...])
    out_ref[...] = (prob * expert_out).astype(jnp.bfloat16)
    d_gate = jnp.sum(expert_out * cot_ref[...].astype(jnp.float32), axis=1, keepdims=True)
    d_gate_ref[...] = jnp.sum(jnp.where(diagonal, d_gate, 0.0), axis=0, keepdims=True)
    stores[0].start()
    stores[2].start()
    for s in steps:
        back(1, s).wait_recv()
    dx_ref[...] = matmul(combine, dx_back[...]).astype(jnp.bfloat16)
    stores[1].start()

    for array in range(2):
        for s in steps:
            go(array, s).wait_send()
            back(array, s).wait_send()
        for kind in range(3):
            for s in range(n):
                forward(array, s, kind).wait_send()
    for store in stores:
        store.wait()


def write_out(*refs):
    made, results, held, sem = refs[:6], refs[6:12], refs[12:18], refs[18]
    reads = [
        pltpu.make_async_copy(src, dst, sem.at[0, i])
        for i, (src, dst) in enumerate(zip(made, held))
    ]
    writes = [
        pltpu.make_async_copy(src, dst, sem.at[1, i])
        for i, (src, dst) in enumerate(zip(held, results))
    ]
    for read in reads:
        read.start()
    for read, write in zip(reads, writes):
        read.wait()
        write.start()
    for write in writes:
        write.wait()


def fused(n, tokens, expert_choice, gate_prob, cotangent, w_gate, w_up, w_down):
    tok, features = tokens.shape
    units = w_gate.shape[1]
    capacity = 3 * tok // (2 * n)
    own = n * capacity
    everyone = 4 * own
    padded = -(-own // LANES) * LANES
    width = features // 4
    bf16, f32 = jnp.bfloat16, jnp.float32
    hbm = pl.BlockSpec(memory_space=pltpu.HBM)
    work = 2 * units * features * (6 * own + 3 * everyone + 3 * own)
    results = pl.pallas_call(
        functools.partial(kernel, n, capacity),
        out_shape=(
            jax.ShapeDtypeStruct((tok, features), bf16),
            jax.ShapeDtypeStruct((tok, features), bf16),
            jax.ShapeDtypeStruct((1, tok), f32),
        )
        + (jax.ShapeDtypeStruct((units, width), bf16),) * 3,
        in_specs=[hbm] * 7,
        out_specs=(hbm,) * 6,
        scratch_shapes=[
            pltpu.VMEM((tok, features), bf16),
            pltpu.VMEM((1, tok), jnp.int32),
            pltpu.VMEM((1, tok), f32),
            pltpu.VMEM((tok, features), bf16),
            pltpu.VMEM((units, features), bf16),
            pltpu.VMEM((units, features), bf16),
            pltpu.VMEM((units, features), bf16),
            pltpu.VMEM((own - capacity, features), bf16),
            pltpu.VMEM((own - capacity, features), bf16),
            pltpu.VMEM((everyone, features), bf16),
            pltpu.VMEM((everyone, features), bf16),
            pltpu.VMEM((own, units), f32),
            pltpu.VMEM((own, units), f32),
            pltpu.VMEM((own, units), bf16),
            pltpu.VMEM((own, units), bf16),
            pltpu.VMEM((own, units), bf16),
            pltpu.VMEM((units, everyone), f32),
            pltpu.VMEM((units, everyone), f32),
            pltpu.VMEM((units, everyone), bf16),
            pltpu.VMEM((own, features), bf16),
            pltpu.VMEM((own, features), bf16),
            pltpu.VMEM((padded, features), bf16),
            pltpu.VMEM((padded, features), bf16),
            pltpu.VMEM((tok, features), bf16),
            pltpu.VMEM((tok, features), bf16),
            pltpu.VMEM((1, tok), f32),
            pltpu.VMEM((units, width), bf16),
            pltpu.VMEM((units, width), bf16),
            pltpu.VMEM((units, width), bf16),
            pltpu.SemaphoreType.DMA((7,)),
            pltpu.SemaphoreType.DMA((6,)),
            pltpu.SemaphoreType.DMA((2, n)),
            pltpu.SemaphoreType.DMA((2, n)),
            pltpu.SemaphoreType.DMA((2, 3, n)),
            pltpu.SemaphoreType.DMA((2, 3, n)),
            pltpu.SemaphoreType.DMA((2, n)),
            pltpu.SemaphoreType.DMA((2, n)),
        ],
        cost_estimate=pl.CostEstimate(
            flops=work, bytes_accessed=6 * units * features, transcendentals=units * everyone
        ),
        compiler_params=pltpu.CompilerParams(
            collective_id=0, has_side_effects=True, vmem_limit_bytes=60 * 1024 * 1024
        ),
    )(
        tokens,
        expert_choice.reshape(1, tok),
        gate_prob.reshape(1, tok),
        cotangent,
        w_gate[0],
        w_up[0],
        w_down[0],
    )
    layer_out, d_tokens, d_gate, *grads = pl.pallas_call(
        write_out,
        out_shape=tuple(jax.ShapeDtypeStruct(r.shape, r.dtype) for r in results),
        in_specs=[hbm] * 6,
        out_specs=(hbm,) * 6,
        scratch_shapes=[pltpu.VMEM(r.shape, r.dtype) for r in results]
        + [pltpu.SemaphoreType.DMA((2, 6))],
        compiler_params=pltpu.CompilerParams(vmem_limit_bytes=60 * 1024 * 1024),
    )(*results)
    return (layer_out, d_tokens, d_gate.reshape(tok, 1), *(grad[None] for grad in grads))


def solution(mesh):
    in_specs = (
        P(("parts", "expert", "dp", "sub"), None),
        P(("parts", "expert", "dp", "sub"), None),
        P(("parts", "expert", "dp", "sub"), None),
        P(("parts", "expert", "dp", "sub"), None),
        P("expert", "sub", None),
        P("expert", "sub", None),
        P("expert", "sub", None),
    )
    out_specs = (
        P(("parts", "expert", "dp", "sub"), None),
        P(("parts", "expert", "dp", "sub"), None),
        P(("parts", "expert", "dp", "sub"), None),
        P(("parts", "expert"), "sub", "dp"),
        P(("parts", "expert"), "sub", "dp"),
        P(("parts", "expert"), "sub", "dp"),
    )
    shape = dict(mesh.shape)
    fits = shape["sub"] == 1 and shape["dp"] == 4

    def device_part(tokens, expert_choice, *rest):
        capacity = 3 * tokens.shape[0] // (2 * shape["expert"])
        one_choice = expert_choice.shape[1] == 1
        if fits and one_choice and tokens.shape[0] == LANES and capacity % 16 == 0:
            return fused(shape["expert"], tokens, expert_choice, *rest)
        return local(tokens, expert_choice, *rest)

    return jax.shard_map(device_part, mesh=mesh, in_specs=in_specs, out_specs=out_specs, check_vma=False)
```

```python
import functools

import jax
import jax.numpy as jnp
from jax import lax
from jax.experimental import pallas as pl
from jax.experimental.pallas import tpu as pltpu
from jax.sharding import PartitionSpec as P


def contract_last(left, right):
    return lax.dot_general(
        left, right, (((1,), (1,)), ((), ())), preferred_element_type=jnp.float32
    )


def contract_rows(left, right):
    return lax.dot_general(
        left, right, (((0,), (0,)), ((), ())), preferred_element_type=jnp.float32
    )


def local(tokens, expert_choice, gate_prob, cotangent, w_gate, w_up, w_down):
    n_expert = lax.axis_size("expert")
    tok_rows, feature_width = tokens.shape
    top_count = expert_choice.shape[1]
    pair_count = tok_rows * top_count
    capacity = 3 * pair_count // (2 * n_expert)
    slot_total = n_expert * capacity
    flat_choice = expert_choice.reshape(pair_count)
    onehot = (flat_choice[:, None] == jnp.arange(n_expert, dtype=jnp.int32)[None, :]).astype(
        jnp.int32
    )
    before = jnp.cumsum(onehot, axis=0) - onehot
    position = jnp.sum(before * onehot, axis=1)
    slot_index = flat_choice * capacity + position
    selector = (slot_index[None, :] == jnp.arange(slot_total, dtype=jnp.int32)[:, None]).astype(
        jnp.bfloat16
    )
    x_pairs = jnp.repeat(tokens, top_count, axis=0)
    cot_pairs = jnp.repeat(cotangent, top_count, axis=0)
    dy_pairs = (gate_prob * cot_pairs.astype(jnp.float32)).astype(jnp.bfloat16)
    x_send = jnp.dot(selector, x_pairs, preferred_element_type=jnp.float32).astype(jnp.bfloat16)
    dy_send = jnp.dot(selector, dy_pairs, preferred_element_type=jnp.float32).astype(jnp.bfloat16)
    weight_gate = w_gate[0]
    weight_up = w_up[0]
    weight_down = w_down[0]
    x_recv, dy_recv = (
        lax.all_to_all(x_send, "expert", split_axis=0, concat_axis=0, tiled=True),
        lax.all_to_all(dy_send, "expert", split_axis=0, concat_axis=0, tiled=True),
    )
    x_rows, dy_rows = (
        lax.all_gather(x_recv, "sub", axis=0, tiled=True),
        lax.all_gather(dy_recv, "sub", axis=0, tiled=True),
    )
    gate_pre = contract_last(x_rows, weight_gate)
    up_pre = contract_last(x_rows, weight_up)
    sigmoid_gate = jax.nn.sigmoid(gate_pre)
    activated = gate_pre * sigmoid_gate
    silu_slope = sigmoid_gate * (1.0 + gate_pre * (1.0 - sigmoid_gate))
    hidden = (activated * up_pre).astype(jnp.bfloat16)
    out_part = jnp.dot(hidden, weight_down, preferred_element_type=jnp.float32)
    d_hidden = contract_last(dy_rows, weight_down)
    grad_down = contract_rows(hidden, dy_rows)
    d_gate_pre = (d_hidden * up_pre * silu_slope).astype(jnp.bfloat16)
    d_up_pre = (d_hidden * activated).astype(jnp.bfloat16)
    dx_part = jnp.dot(d_gate_pre, weight_gate, preferred_element_type=jnp.float32) + jnp.dot(
        d_up_pre, weight_up, preferred_element_type=jnp.float32
    )
    grad_gate = contract_rows(d_gate_pre, x_rows)
    grad_up = contract_rows(d_up_pre, x_rows)
    summed_gate = lax.psum_scatter(
        grad_gate.astype(jnp.bfloat16), "dp", scatter_dimension=1, tiled=True
    ).astype(jnp.float32)
    summed_up = lax.psum_scatter(
        grad_up.astype(jnp.bfloat16), "dp", scatter_dimension=1, tiled=True
    ).astype(jnp.float32)
    summed_down = lax.psum_scatter(
        grad_down.astype(jnp.bfloat16), "dp", scatter_dimension=1, tiled=True
    ).astype(jnp.float32)
    out_part, dx_part, summed = (out_part, dx_part, (summed_gate, summed_up, summed_down))
    out_mine, dx_mine = (
        lax.psum_scatter(
            out_part.astype(jnp.bfloat16), "sub", scatter_dimension=0, tiled=True
        ).astype(jnp.float32),
        lax.psum_scatter(
            dx_part.astype(jnp.bfloat16), "sub", scatter_dimension=0, tiled=True
        ).astype(jnp.float32),
    )
    out_back, dx_back = (
        lax.all_to_all(
            out_mine.astype(jnp.bfloat16), "expert", split_axis=0, concat_axis=0, tiled=True
        ),
        lax.all_to_all(
            dx_mine.astype(jnp.bfloat16), "expert", split_axis=0, concat_axis=0, tiled=True
        ),
    )
    out_three = contract_rows(selector, out_back).reshape(tok_rows, top_count, feature_width)
    dx_three = contract_rows(selector, dx_back).reshape(tok_rows, top_count, feature_width)
    layer_out = jnp.sum(gate_prob[:, :, None] * out_three, axis=1).astype(jnp.bfloat16)
    d_gate = jnp.sum(out_three * cotangent[:, None, :].astype(jnp.float32), axis=2)
    d_tokens = jnp.sum(dx_three, axis=1).astype(jnp.bfloat16)
    summed_gate, summed_up, summed_down = summed
    return (
        layer_out,
        d_tokens,
        d_gate,
        summed_gate.astype(jnp.bfloat16)[None],
        summed_up.astype(jnp.bfloat16)[None],
        summed_down.astype(jnp.bfloat16)[None],
    )


LANES = 128
BLOCK = 256
MESH = pl.DeviceIdType.MESH


def matmul(left, right):
    return jnp.dot(left, right, preferred_element_type=jnp.float32)


def kernel(
    n, capacity,
    tokens_hbm, choice_hbm, prob_hbm, cot_hbm, w_gate_hbm, w_up_hbm, w_down_hbm,
    out_hbm, dx_hbm, d_gate_hbm, grad_gate_hbm, grad_up_hbm, grad_down_hbm,
    tokens_ref, choice_ref, prob_ref, cot_ref,
    w_gate, w_up, w_down, x_send, y_send, x_all, y_all,
    active, slope, hidden, d_gate_pre, d_up_pre,
    active_t, slope_t, hidden_t, out_rows, dx_rows, out_back, dx_back,
    out_ref, dx_ref, d_gate_ref, grad_gate_ref, grad_up_ref, grad_down_ref,
    load_sem, store_sem, go_sem, go_recv, fwd_sem, fwd_recv, back_sem, back_recv,
):
    loads = [
        pltpu.make_async_copy(src, dst, load_sem.at[i])
        for i, (src, dst) in enumerate(
            (
                (choice_hbm, choice_ref),
                (tokens_hbm, tokens_ref),
                (prob_hbm, prob_ref),
                (cot_hbm, cot_ref),
                (w_gate_hbm, w_gate),
                (w_up_hbm, w_up),
                (w_down_hbm, w_down),
            )
        )
    ]
    for load in loads:
        load.start()
    stores = [
        pltpu.make_async_copy(src, dst, store_sem.at[i])
        for i, (src, dst) in enumerate(
            (
                (out_ref, out_hbm),
                (dx_ref, dx_hbm),
                (d_gate_ref, d_gate_hbm),
                (grad_gate_ref, grad_gate_hbm),
                (grad_up_ref, grad_up_hbm),
                (grad_down_ref, grad_down_hbm),
            )
        )
    ]
    me = lax.axis_index("expert")
    dp = lax.axis_index("dp")
    sibling = dp + 1 - 2 * lax.rem(dp, 2)
    across = lax.rem(dp + 2, 4)
    peers = [lax.rem(me + s, n) for s in range(n)]
    sources = [lax.rem(me + n - s, n) for s in range(n)]
    own = n * capacity
    units = w_gate.shape[0]
    features = w_gate.shape[1]
    steps = range(n - 1, 0, -1)

    barrier = pltpu.get_barrier_semaphore()
    for s in steps:
        pl.semaphore_signal(barrier, inc=1, device_id={"expert": peers[s]}, device_id_type=MESH)
    for d in (sibling, across):
        pl.semaphore_signal(barrier, inc=1, device_id={"dp": d}, device_id_type=MESH)

    loads[0].wait()
    choice = choice_ref[...]
    relative = choice - me
    relative = jnp.where(relative < 0, relative + n, relative)
    tok = LANES
    row_id = lax.broadcasted_iota(jnp.int32, (tok, tok), 0)
    col_id = lax.broadcasted_iota(jnp.int32, (tok, tok), 1)
    earlier = (row_id < col_id).astype(jnp.bfloat16)
    expert_rows = max(16, n)
    onehot = lax.broadcasted_iota(jnp.int32, (expert_rows, tok), 0) == relative
    before = matmul(onehot.astype(jnp.bfloat16), earlier)
    position = jnp.sum(jnp.where(onehot, before, 0.0), axis=0, keepdims=True)
    slot = relative * capacity + position.astype(jnp.int32)
    selector = (
        lax.broadcasted_iota(jnp.int32, (own, tok), 0) == slot
    ).astype(jnp.bfloat16)
    diagonal = row_id == col_id

    def rows(s, group=0):
        return pl.ds(group * own + s * capacity, capacity)

    def dispatch(values, buffer, held, array):
        picked = matmul(selector, values).astype(jnp.bfloat16)
        held[pl.ds(0, capacity), :] = picked[:capacity]
        buffer[...] = picked[capacity:]

    def go(array, s):
        buffer, held = ((x_send, x_all), (y_send, y_all))[array]
        return pltpu.make_async_remote_copy(
            src_ref=buffer.at[pl.ds((s - 1) * capacity, capacity)],
            dst_ref=held.at[rows(s)],
            send_sem=go_sem.at[array, s],
            recv_sem=go_recv.at[array, s],
            device_id={"expert": peers[s]},
            device_id_type=MESH,
        )

    def forward(array, s, kind):
        held = (x_all, y_all)[array]
        came, lands, target = ((0, 1, sibling), (0, 2, across), (2, 3, sibling))[kind]
        return pltpu.make_async_remote_copy(
            src_ref=held.at[rows(s, came)],
            dst_ref=held.at[rows(s, lands)],
            send_sem=fwd_sem.at[array, kind, s],
            recv_sem=fwd_recv.at[array, kind, s],
            device_id={"dp": target},
            device_id_type=MESH,
        )

    def back(array, s):
        made, held = ((out_rows, out_back), (dx_rows, dx_back))[array]
        return pltpu.make_async_remote_copy(
            src_ref=made.at[rows(s)],
            dst_ref=held.at[rows(s)],
            send_sem=back_sem.at[array, s],
            recv_sem=back_recv.at[array, s],
            device_id={"expert": sources[s]},
            device_id_type=MESH,
        )

    loads[1].wait()
    dispatch(tokens_ref[...], x_send, x_all, 0)
    pl.semaphore_wait(barrier, n + 1)
    for s in steps:
        go(0, s).start()
    forward(0, 0, 1).start()
    forward(0, 0, 0).start()
    loads[2].wait()
    loads[3].wait()
    prob = jnp.sum(jnp.where(diagonal, prob_ref[...], 0.0), axis=1, keepdims=True)
    scaled = (prob * cot_ref[...].astype(jnp.float32)).astype(jnp.bfloat16)
    dispatch(scaled, y_send, y_all, 1)
    for s in steps:
        go(1, s).start()
    forward(1, 0, 1).start()
    forward(1, 0, 0).start()

    tail = out_back.shape[0] - own
    if tail:
        out_back[pl.ds(own, tail), :] = jnp.zeros((tail, features), jnp.bfloat16)
        dx_back[pl.ds(own, tail), :] = jnp.zeros((tail, features), jnp.bfloat16)
    for load in loads[4:]:
        load.wait()

    for s in steps:
        go(0, s).wait_recv()
        forward(0, s, 1).start()
        forward(0, s, 0).start()

    def parts_of(gate_pre, up_pre):
        sigmoid = jax.nn.sigmoid(gate_pre)
        activated = gate_pre * sigmoid
        sloped = up_pre * (sigmoid * (1.0 + gate_pre * (1.0 - sigmoid)))
        return activated, sloped, (activated * up_pre).astype(jnp.bfloat16)

    mine = pl.ds(0, own)

    def own_forward(u, carry):
        cut = pl.ds(pl.multiple_of(u * BLOCK, BLOCK), BLOCK)
        x = x_all[mine, :]
        activated, sloped, made = parts_of(
            contract_last(x, w_gate[cut, :]), contract_last(x, w_up[cut, :])
        )
        active[:, cut] = activated
        slope[:, cut] = sloped
        hidden[:, cut] = made
        return carry

    lax.fori_loop(0, units // BLOCK, own_forward, 0)

    def own_out(j, carry):
        cut = pl.ds(pl.multiple_of(j * BLOCK, BLOCK), BLOCK)
        out_rows[:, cut] = matmul(hidden[...], w_down[:, cut]).astype(jnp.bfloat16)
        return carry

    lax.fori_loop(0, features // BLOCK, own_out, 0)
    for s in steps:
        back(0, s).start()
    out_back[pl.ds(0, capacity), :] = out_rows[pl.ds(0, capacity), :]

    for s in range(n):
        forward(0, s, 1).wait_recv()
        forward(0, s, 2).start()
    for kind in (0, 2):
        for s in range(n):
            forward(0, s, kind).wait_recv()

    def all_forward(u, carry):
        cut = pl.ds(pl.multiple_of(u * BLOCK, BLOCK), BLOCK)
        x = x_all[...]
        activated, sloped, made = parts_of(
            contract_last(w_gate[cut, :], x), contract_last(w_up[cut, :], x)
        )
        active_t[cut, :] = activated
        slope_t[cut, :] = sloped
        hidden_t[cut, :] = made
        return carry

    lax.fori_loop(0, units // BLOCK - 1, all_forward, 0)

    for s in steps:
        go(1, s).wait_recv()
        forward(1, s, 1).start()
        forward(1, s, 0).start()

    def own_backward(u, carry):
        cut = pl.ds(pl.multiple_of(u * BLOCK, BLOCK), BLOCK)
        d_hidden = contract_last(y_all[mine, :], w_down[cut, :])
        d_gate_pre[:, cut] = (d_hidden * slope[:, cut]).astype(jnp.bfloat16)
        d_up_pre[:, cut] = (d_hidden * active[:, cut]).astype(jnp.bfloat16)
        return carry

    lax.fori_loop(0, units // BLOCK, own_backward, 0)

    def own_dx(j, carry):
        cut = pl.ds(pl.multiple_of(j * BLOCK, BLOCK), BLOCK)
        dx_rows[:, cut] = (
            matmul(d_gate_pre[...], w_gate[:, cut]) + matmul(d_up_pre[...], w_up[:, cut])
        ).astype(jnp.bfloat16)
        return carry

    lax.fori_loop(0, features // BLOCK, own_dx, 0)
    for s in steps:
        back(1, s).start()
    dx_back[pl.ds(0, capacity), :] = dx_rows[pl.ds(0, capacity), :]
    lax.fori_loop(units // BLOCK - 1, units // BLOCK, all_forward, 0)

    for s in range(n):
        forward(1, s, 1).wait_recv()
        forward(1, s, 2).start()
    for kind in (0, 2):
        for s in range(n):
            forward(1, s, kind).wait_recv()

    width = grad_gate_ref.shape[1]
    columns = pl.ds(pl.multiple_of(dp * width, width), width)

    def all_backward(u, carry):
        cut = pl.ds(pl.multiple_of(u * BLOCK, BLOCK), BLOCK)
        d_hidden = contract_last(w_down[cut, :], y_all[...])
        left_gate = (d_hidden * slope_t[cut, :]).astype(jnp.bfloat16)
        left_up = (d_hidden * active_t[cut, :]).astype(jnp.bfloat16)
        x = x_all[:, columns]
        grad_gate_ref[cut, :] = matmul(left_gate, x).astype(jnp.bfloat16)
        grad_up_ref[cut, :] = matmul(left_up, x).astype(jnp.bfloat16)
        grad_down_ref[cut, :] = matmul(hidden_t[cut, :], y_all[:, columns]).astype(jnp.bfloat16)
        return carry

    lax.fori_loop(0, units // BLOCK, all_backward, 0)

    for store in stores[3:]:
        store.start()
    slot_column = jnp.sum(jnp.where(diagonal, slot, 0), axis=1, keepdims=True)
    combine = (
        lax.broadcasted_iota(jnp.int32, (tok, out_back.shape[0]), 1) == slot_column
    ).astype(jnp.bfloat16)
    for s in steps:
        back(0, s).wait_recv()
    expert_out = matmul(combine, out_back[...])
    out_ref[...] = (prob * expert_out).astype(jnp.bfloat16)
    d_gate = jnp.sum(expert_out * cot_ref[...].astype(jnp.float32), axis=1, keepdims=True)
    d_gate_ref[...] = jnp.sum(jnp.where(diagonal, d_gate, 0.0), axis=0, keepdims=True)
    stores[0].start()
    stores[2].start()
    for s in steps:
        back(1, s).wait_recv()
    dx_ref[...] = matmul(combine, dx_back[...]).astype(jnp.bfloat16)
    stores[1].start()

    for array in range(2):
        for s in steps:
            go(array, s).wait_send()
            back(array, s).wait_send()
        for kind in range(3):
            for s in range(n):
                forward(array, s, kind).wait_send()
    for store in stores:
        store.wait()


def write_out(*refs):
    made, results, held, sem = refs[:6], refs[6:12], refs[12:18], refs[18]
    reads = [
        pltpu.make_async_copy(src, dst, sem.at[0, i])
        for i, (src, dst) in enumerate(zip(made, held))
    ]
    writes = [
        pltpu.make_async_copy(src, dst, sem.at[1, i])
        for i, (src, dst) in enumerate(zip(held, results))
    ]
    for read in reads:
        read.start()
    for read, write in zip(reads, writes):
        read.wait()
        write.start()
    for write in writes:
        write.wait()


def fused(n, tokens, expert_choice, gate_prob, cotangent, w_gate, w_up, w_down):
    tok, features = tokens.shape
    units = w_gate.shape[1]
    capacity = 3 * tok // (2 * n)
    own = n * capacity
    everyone = 4 * own
    padded = -(-own // LANES) * LANES
    width = features // 4
    bf16, f32 = jnp.bfloat16, jnp.float32
    hbm = pl.BlockSpec(memory_space=pltpu.HBM)
    work = 2 * units * features * (6 * own + 3 * everyone + 3 * own)
    results = pl.pallas_call(
        functools.partial(kernel, n, capacity),
        out_shape=(
            jax.ShapeDtypeStruct((tok, features), bf16),
            jax.ShapeDtypeStruct((tok, features), bf16),
            jax.ShapeDtypeStruct((1, tok), f32),
        )
        + (jax.ShapeDtypeStruct((units, width), bf16),) * 3,
        in_specs=[hbm] * 7,
        out_specs=(hbm,) * 6,
        scratch_shapes=[
            pltpu.VMEM((tok, features), bf16),
            pltpu.VMEM((1, tok), jnp.int32),
            pltpu.VMEM((1, tok), f32),
            pltpu.VMEM((tok, features), bf16),
            pltpu.VMEM((units, features), bf16),
            pltpu.VMEM((units, features), bf16),
            pltpu.VMEM((units, features), bf16),
            pltpu.VMEM((own - capacity, features), bf16),
            pltpu.VMEM((own - capacity, features), bf16),
            pltpu.VMEM((everyone, features), bf16),
            pltpu.VMEM((everyone, features), bf16),
            pltpu.VMEM((own, units), f32),
            pltpu.VMEM((own, units), f32),
            pltpu.VMEM((own, units), bf16),
            pltpu.VMEM((own, units), bf16),
            pltpu.VMEM((own, units), bf16),
            pltpu.VMEM((units, everyone), f32),
            pltpu.VMEM((units, everyone), f32),
            pltpu.VMEM((units, everyone), bf16),
            pltpu.VMEM((own, features), bf16),
            pltpu.VMEM((own, features), bf16),
            pltpu.VMEM((padded, features), bf16),
            pltpu.VMEM((padded, features), bf16),
            pltpu.VMEM((tok, features), bf16),
            pltpu.VMEM((tok, features), bf16),
            pltpu.VMEM((1, tok), f32),
            pltpu.VMEM((units, width), bf16),
            pltpu.VMEM((units, width), bf16),
            pltpu.VMEM((units, width), bf16),
            pltpu.SemaphoreType.DMA((7,)),
            pltpu.SemaphoreType.DMA((6,)),
            pltpu.SemaphoreType.DMA((2, n)),
            pltpu.SemaphoreType.DMA((2, n)),
            pltpu.SemaphoreType.DMA((2, 3, n)),
            pltpu.SemaphoreType.DMA((2, 3, n)),
            pltpu.SemaphoreType.DMA((2, n)),
            pltpu.SemaphoreType.DMA((2, n)),
        ],
        cost_estimate=pl.CostEstimate(
            flops=work, bytes_accessed=6 * units * features, transcendentals=units * everyone
        ),
        compiler_params=pltpu.CompilerParams(
            collective_id=0, has_side_effects=True, vmem_limit_bytes=60 * 1024 * 1024
        ),
    )(
        tokens,
        expert_choice.reshape(1, tok),
        gate_prob.reshape(1, tok),
        cotangent,
        w_gate[0],
        w_up[0],
        w_down[0],
    )
    layer_out, d_tokens, d_gate, *grads = pl.pallas_call(
        write_out,
        out_shape=tuple(jax.ShapeDtypeStruct(r.shape, r.dtype) for r in results),
        in_specs=[hbm] * 6,
        out_specs=(hbm,) * 6,
        scratch_shapes=[pltpu.VMEM(r.shape, r.dtype) for r in results]
        + [pltpu.SemaphoreType.DMA((2, 6))],
        compiler_params=pltpu.CompilerParams(vmem_limit_bytes=60 * 1024 * 1024),
    )(*results)
    return (layer_out, d_tokens, d_gate.reshape(tok, 1), *(grad[None] for grad in grads))


def solution(mesh):
    in_specs = (
        P(("parts", "expert", "dp", "sub"), None),
        P(("parts", "expert", "dp", "sub"), None),
        P(("parts", "expert", "dp", "sub"), None),
        P(("parts", "expert", "dp", "sub"), None),
        P("expert", "sub", None),
        P("expert", "sub", None),
        P("expert", "sub", None),
    )
    out_specs = (
        P(("parts", "expert", "dp", "sub"), None),
        P(("parts", "expert", "dp", "sub"), None),
        P(("parts", "expert", "dp", "sub"), None),
        P(("parts", "expert"), "sub", "dp"),
        P(("parts", "expert"), "sub", "dp"),
        P(("parts", "expert"), "sub", "dp"),
    )
    shape = dict(mesh.shape)
    fits = shape["sub"] == 1 and shape["dp"] == 4

    def device_part(tokens, expert_choice, *rest):
        capacity = 3 * tokens.shape[0] // (2 * shape["expert"])
        one_choice = expert_choice.shape[1] == 1
        if fits and one_choice and tokens.shape[0] == LANES and capacity % 16 == 0:
            return fused(shape["expert"], tokens, expert_choice, *rest)
        return local(tokens, expert_choice, *rest)

    return jax.shard_map(device_part, mesh=mesh, in_specs=in_specs, out_specs=out_specs, check_vma=False)
```

```python
import functools

import jax
import jax.numpy as jnp
from jax import lax
from jax.experimental import pallas as pl
from jax.experimental.pallas import tpu as pltpu
from jax.sharding import PartitionSpec as P


def contract_last(left, right):
    return lax.dot_general(
        left, right, (((1,), (1,)), ((), ())), preferred_element_type=jnp.float32
    )


def contract_rows(left, right):
    return lax.dot_general(
        left, right, (((0,), (0,)), ((), ())), preferred_element_type=jnp.float32
    )


def local(tokens, expert_choice, gate_prob, cotangent, w_gate, w_up, w_down):
    n_expert = lax.axis_size("expert")
    tok_rows, feature_width = tokens.shape
    top_count = expert_choice.shape[1]
    pair_count = tok_rows * top_count
    capacity = 3 * pair_count // (2 * n_expert)
    slot_total = n_expert * capacity
    flat_choice = expert_choice.reshape(pair_count)
    onehot = (flat_choice[:, None] == jnp.arange(n_expert, dtype=jnp.int32)[None, :]).astype(
        jnp.int32
    )
    before = jnp.cumsum(onehot, axis=0) - onehot
    position = jnp.sum(before * onehot, axis=1)
    slot_index = flat_choice * capacity + position
    selector = (slot_index[None, :] == jnp.arange(slot_total, dtype=jnp.int32)[:, None]).astype(
        jnp.bfloat16
    )
    x_pairs = jnp.repeat(tokens, top_count, axis=0)
    cot_pairs = jnp.repeat(cotangent, top_count, axis=0)
    dy_pairs = (gate_prob * cot_pairs.astype(jnp.float32)).astype(jnp.bfloat16)
    x_send = jnp.dot(selector, x_pairs, preferred_element_type=jnp.float32).astype(jnp.bfloat16)
    dy_send = jnp.dot(selector, dy_pairs, preferred_element_type=jnp.float32).astype(jnp.bfloat16)
    weight_gate = w_gate[0]
    weight_up = w_up[0]
    weight_down = w_down[0]
    x_recv, dy_recv = (
        lax.all_to_all(x_send, "expert", split_axis=0, concat_axis=0, tiled=True),
        lax.all_to_all(dy_send, "expert", split_axis=0, concat_axis=0, tiled=True),
    )
    x_rows, dy_rows = (
        lax.all_gather(x_recv, "sub", axis=0, tiled=True),
        lax.all_gather(dy_recv, "sub", axis=0, tiled=True),
    )
    gate_pre = contract_last(x_rows, weight_gate)
    up_pre = contract_last(x_rows, weight_up)
    sigmoid_gate = jax.nn.sigmoid(gate_pre)
    activated = gate_pre * sigmoid_gate
    silu_slope = sigmoid_gate * (1.0 + gate_pre * (1.0 - sigmoid_gate))
    hidden = (activated * up_pre).astype(jnp.bfloat16)
    out_part = jnp.dot(hidden, weight_down, preferred_element_type=jnp.float32)
    d_hidden = contract_last(dy_rows, weight_down)
    grad_down = contract_rows(hidden, dy_rows)
    d_gate_pre = (d_hidden * up_pre * silu_slope).astype(jnp.bfloat16)
    d_up_pre = (d_hidden * activated).astype(jnp.bfloat16)
    dx_part = jnp.dot(d_gate_pre, weight_gate, preferred_element_type=jnp.float32) + jnp.dot(
        d_up_pre, weight_up, preferred_element_type=jnp.float32
    )
    grad_gate = contract_rows(d_gate_pre, x_rows)
    grad_up = contract_rows(d_up_pre, x_rows)
    summed_gate = lax.psum_scatter(
        grad_gate.astype(jnp.bfloat16), "dp", scatter_dimension=1, tiled=True
    ).astype(jnp.float32)
    summed_up = lax.psum_scatter(
        grad_up.astype(jnp.bfloat16), "dp", scatter_dimension=1, tiled=True
    ).astype(jnp.float32)
    summed_down = lax.psum_scatter(
        grad_down.astype(jnp.bfloat16), "dp", scatter_dimension=1, tiled=True
    ).astype(jnp.float32)
    out_part, dx_part, summed = (out_part, dx_part, (summed_gate, summed_up, summed_down))
    out_mine, dx_mine = (
        lax.psum_scatter(
            out_part.astype(jnp.bfloat16), "sub", scatter_dimension=0, tiled=True
        ).astype(jnp.float32),
        lax.psum_scatter(
            dx_part.astype(jnp.bfloat16), "sub", scatter_dimension=0, tiled=True
        ).astype(jnp.float32),
    )
    out_back, dx_back = (
        lax.all_to_all(
            out_mine.astype(jnp.bfloat16), "expert", split_axis=0, concat_axis=0, tiled=True
        ),
        lax.all_to_all(
            dx_mine.astype(jnp.bfloat16), "expert", split_axis=0, concat_axis=0, tiled=True
        ),
    )
    out_three = contract_rows(selector, out_back).reshape(tok_rows, top_count, feature_width)
    dx_three = contract_rows(selector, dx_back).reshape(tok_rows, top_count, feature_width)
    layer_out = jnp.sum(gate_prob[:, :, None] * out_three, axis=1).astype(jnp.bfloat16)
    d_gate = jnp.sum(out_three * cotangent[:, None, :].astype(jnp.float32), axis=2)
    d_tokens = jnp.sum(dx_three, axis=1).astype(jnp.bfloat16)
    summed_gate, summed_up, summed_down = summed
    return (
        layer_out,
        d_tokens,
        d_gate,
        summed_gate.astype(jnp.bfloat16)[None],
        summed_up.astype(jnp.bfloat16)[None],
        summed_down.astype(jnp.bfloat16)[None],
    )


LANES = 128
BLOCK = 256
MESH = pl.DeviceIdType.MESH


def matmul(left, right):
    return jnp.dot(left, right, preferred_element_type=jnp.float32)


def kernel(
    n, capacity,
    tokens_hbm, choice_hbm, prob_hbm, cot_hbm, w_gate_hbm, w_up_hbm, w_down_hbm,
    out_hbm, dx_back, combine_hbm, d_gate_hbm, grad_gate_hbm, grad_up_hbm, grad_down_hbm,
    tokens_ref, choice_ref, prob_ref, cot_ref,
    w_gate, w_up, w_down, x_send, y_send, x_all, y_all,
    active, slope, hidden, d_gate_pre, d_up_pre,
    active_t, slope_t, hidden_t, out_rows, dx_rows, out_back,
    out_ref, combine_ref, d_gate_ref, grad_gate_ref, grad_up_ref, grad_down_ref,
    load_sem, store_sem, go_sem, go_recv, fwd_sem, fwd_recv, back_sem, back_recv,
):
    loads = [
        pltpu.make_async_copy(src, dst, load_sem.at[i])
        for i, (src, dst) in enumerate(
            (
                (choice_hbm, choice_ref),
                (tokens_hbm, tokens_ref),
                (prob_hbm, prob_ref),
                (cot_hbm, cot_ref),
                (w_gate_hbm, w_gate),
                (w_up_hbm, w_up),
                (w_down_hbm, w_down),
            )
        )
    ]
    for load in loads:
        load.start()
    stores = [
        pltpu.make_async_copy(src, dst, store_sem.at[i])
        for i, (src, dst) in enumerate(
            (
                (out_ref, out_hbm),
                (combine_ref, combine_hbm),
                (d_gate_ref, d_gate_hbm),
                (grad_gate_ref, grad_gate_hbm),
                (grad_up_ref, grad_up_hbm),
                (grad_down_ref, grad_down_hbm),
                (dx_rows.at[pl.ds(0, capacity)], dx_back.at[pl.ds(0, capacity)]),
            )
        )
    ]
    me = lax.axis_index("expert")
    dp = lax.axis_index("dp")
    sibling = dp + 1 - 2 * lax.rem(dp, 2)
    across = lax.rem(dp + 2, 4)
    peers = [lax.rem(me + s, n) for s in range(n)]
    sources = [lax.rem(me + n - s, n) for s in range(n)]
    own = n * capacity
    units = w_gate.shape[0]
    features = w_gate.shape[1]
    steps = range(n - 1, 0, -1)

    barrier = pltpu.get_barrier_semaphore()
    for s in steps:
        pl.semaphore_signal(barrier, inc=1, device_id={"expert": peers[s]}, device_id_type=MESH)
    for d in (sibling, across):
        pl.semaphore_signal(barrier, inc=1, device_id={"dp": d}, device_id_type=MESH)

    loads[0].wait()
    choice = choice_ref[...]
    relative = choice - me
    relative = jnp.where(relative < 0, relative + n, relative)
    tok = LANES
    row_id = lax.broadcasted_iota(jnp.int32, (tok, tok), 0)
    col_id = lax.broadcasted_iota(jnp.int32, (tok, tok), 1)
    earlier = (row_id < col_id).astype(jnp.bfloat16)
    expert_rows = max(16, n)
    onehot = lax.broadcasted_iota(jnp.int32, (expert_rows, tok), 0) == relative
    before = matmul(onehot.astype(jnp.bfloat16), earlier)
    position = jnp.sum(jnp.where(onehot, before, 0.0), axis=0, keepdims=True)
    slot = relative * capacity + position.astype(jnp.int32)
    selector = (
        lax.broadcasted_iota(jnp.int32, (own, tok), 0) == slot
    ).astype(jnp.bfloat16)
    diagonal = row_id == col_id

    def rows(s, group=0):
        return pl.ds(group * own + s * capacity, capacity)

    def dispatch(values, buffer, held, array):
        picked = matmul(selector, values).astype(jnp.bfloat16)
        held[pl.ds(0, capacity), :] = picked[:capacity]
        buffer[...] = picked[capacity:]

    def go(array, s):
        buffer, held = ((x_send, x_all), (y_send, y_all))[array]
        return pltpu.make_async_remote_copy(
            src_ref=buffer.at[pl.ds((s - 1) * capacity, capacity)],
            dst_ref=held.at[rows(s)],
            send_sem=go_sem.at[array, s],
            recv_sem=go_recv.at[array, s],
            device_id={"expert": peers[s]},
            device_id_type=MESH,
        )

    def forward(array, s, kind):
        held = (x_all, y_all)[array]
        came, lands, target = ((0, 1, sibling), (0, 2, across), (2, 3, sibling))[kind]
        return pltpu.make_async_remote_copy(
            src_ref=held.at[rows(s, came)],
            dst_ref=held.at[rows(s, lands)],
            send_sem=fwd_sem.at[array, kind, s],
            recv_sem=fwd_recv.at[array, kind, s],
            device_id={"dp": target},
            device_id_type=MESH,
        )

    def back(array, s):
        made, held = ((out_rows, out_back), (dx_rows, dx_back))[array]
        return pltpu.make_async_remote_copy(
            src_ref=made.at[rows(s)],
            dst_ref=held.at[rows(s)],
            send_sem=back_sem.at[array, s],
            recv_sem=back_recv.at[array, s],
            device_id={"expert": sources[s]},
            device_id_type=MESH,
        )

    loads[1].wait()
    dispatch(tokens_ref[...], x_send, x_all, 0)
    pl.semaphore_wait(barrier, n + 1)
    for s in steps:
        go(0, s).start()
    forward(0, 0, 1).start()
    forward(0, 0, 0).start()
    loads[2].wait()
    loads[3].wait()
    prob = jnp.sum(jnp.where(diagonal, prob_ref[...], 0.0), axis=1, keepdims=True)
    scaled = (prob * cot_ref[...].astype(jnp.float32)).astype(jnp.bfloat16)
    dispatch(scaled, y_send, y_all, 1)
    for s in steps:
        go(1, s).start()
    forward(1, 0, 1).start()
    forward(1, 0, 0).start()

    tail = out_back.shape[0] - own
    if tail:
        out_back[pl.ds(own, tail), :] = jnp.zeros((tail, features), jnp.bfloat16)
    for load in loads[4:]:
        load.wait()

    for s in steps:
        go(0, s).wait_recv()
        forward(0, s, 1).start()
        forward(0, s, 0).start()

    def parts_of(gate_pre, up_pre):
        sigmoid = jax.nn.sigmoid(gate_pre)
        activated = gate_pre * sigmoid
        sloped = up_pre * (sigmoid * (1.0 + gate_pre * (1.0 - sigmoid)))
        return activated, sloped, (activated * up_pre).astype(jnp.bfloat16)

    mine = pl.ds(0, own)

    def own_forward(u, carry):
        cut = pl.ds(pl.multiple_of(u * BLOCK, BLOCK), BLOCK)
        x = x_all[mine, :]
        activated, sloped, made = parts_of(
            contract_last(x, w_gate[cut, :]), contract_last(x, w_up[cut, :])
        )
        active[:, cut] = activated
        slope[:, cut] = sloped
        hidden[:, cut] = made
        return carry

    lax.fori_loop(0, units // BLOCK, own_forward, 0)

    def own_out(j, carry):
        cut = pl.ds(pl.multiple_of(j * BLOCK, BLOCK), BLOCK)
        out_rows[:, cut] = matmul(hidden[...], w_down[:, cut]).astype(jnp.bfloat16)
        return carry

    lax.fori_loop(0, features // BLOCK, own_out, 0)
    for s in steps:
        back(0, s).start()
    out_back[pl.ds(0, capacity), :] = out_rows[pl.ds(0, capacity), :]

    for s in range(n):
        forward(0, s, 1).wait_recv()
        forward(0, s, 2).start()
    for kind in (0, 2):
        for s in range(n):
            forward(0, s, kind).wait_recv()

    def all_forward(u, carry):
        cut = pl.ds(pl.multiple_of(u * BLOCK, BLOCK), BLOCK)
        x = x_all[...]
        activated, sloped, made = parts_of(
            contract_last(w_gate[cut, :], x), contract_last(w_up[cut, :], x)
        )
        active_t[cut, :] = activated
        slope_t[cut, :] = sloped
        hidden_t[cut, :] = made
        return carry

    lax.fori_loop(0, units // BLOCK - 1, all_forward, 0)

    for s in steps:
        go(1, s).wait_recv()
        forward(1, s, 1).start()
        forward(1, s, 0).start()

    def own_backward(u, carry):
        cut = pl.ds(pl.multiple_of(u * BLOCK, BLOCK), BLOCK)
        d_hidden = contract_last(y_all[mine, :], w_down[cut, :])
        d_gate_pre[:, cut] = (d_hidden * slope[:, cut]).astype(jnp.bfloat16)
        d_up_pre[:, cut] = (d_hidden * active[:, cut]).astype(jnp.bfloat16)
        return carry

    lax.fori_loop(0, units // BLOCK, own_backward, 0)

    def own_dx(j, carry):
        cut = pl.ds(pl.multiple_of(j * BLOCK, BLOCK), BLOCK)
        dx_rows[:, cut] = (
            matmul(d_gate_pre[...], w_gate[:, cut]) + matmul(d_up_pre[...], w_up[:, cut])
        ).astype(jnp.bfloat16)
        return carry

    lax.fori_loop(0, features // BLOCK, own_dx, 0)
    for s in steps:
        back(1, s).start()
    stores[6].start()
    lax.fori_loop(units // BLOCK - 1, units // BLOCK, all_forward, 0)

    for s in range(n):
        forward(1, s, 1).wait_recv()
        forward(1, s, 2).start()
    for kind in (0, 2):
        for s in range(n):
            forward(1, s, kind).wait_recv()

    width = grad_gate_ref.shape[1]
    columns = pl.ds(pl.multiple_of(dp * width, width), width)

    def all_backward(u, carry):
        cut = pl.ds(pl.multiple_of(u * BLOCK, BLOCK), BLOCK)
        d_hidden = contract_last(w_down[cut, :], y_all[...])
        left_gate = (d_hidden * slope_t[cut, :]).astype(jnp.bfloat16)
        left_up = (d_hidden * active_t[cut, :]).astype(jnp.bfloat16)
        x = x_all[:, columns]
        grad_gate_ref[cut, :] = matmul(left_gate, x).astype(jnp.bfloat16)
        grad_up_ref[cut, :] = matmul(left_up, x).astype(jnp.bfloat16)
        grad_down_ref[cut, :] = matmul(hidden_t[cut, :], y_all[:, columns]).astype(jnp.bfloat16)
        return carry

    lax.fori_loop(0, units // BLOCK, all_backward, 0)

    for store in stores[3:6]:
        store.start()
    slot_column = jnp.sum(jnp.where(diagonal, slot, 0), axis=1, keepdims=True)
    combine = (
        lax.broadcasted_iota(jnp.int32, (tok, out_back.shape[0]), 1) == slot_column
    ).astype(jnp.bfloat16)
    combine_ref[...] = combine
    stores[1].start()
    for s in steps:
        back(0, s).wait_recv()
    expert_out = matmul(combine, out_back[...])
    out_ref[...] = (prob * expert_out).astype(jnp.bfloat16)
    d_gate = jnp.sum(expert_out * cot_ref[...].astype(jnp.float32), axis=1, keepdims=True)
    d_gate_ref[...] = jnp.sum(jnp.where(diagonal, d_gate, 0.0), axis=0, keepdims=True)
    stores[0].start()
    stores[2].start()
    for s in steps:
        back(1, s).wait_recv()

    for array in range(2):
        for s in steps:
            go(array, s).wait_send()
            back(array, s).wait_send()
        for kind in range(3):
            for s in range(n):
                forward(array, s, kind).wait_send()
    for store in stores:
        store.wait()


def write_out(*refs):
    made, results, held, dx_ref, sem = refs[:7], refs[7:13], refs[13:20], refs[20], refs[21]
    dx_held, combine_held = held[:2]
    own = made[0].shape[0]
    tail = dx_held.shape[0] - own
    landing = (dx_held.at[pl.ds(0, own)],) + tuple(held[1:])
    reads = [
        pltpu.make_async_copy(src, dst, sem.at[0, i])
        for i, (src, dst) in enumerate(zip(made, landing))
    ]
    sources = (dx_ref,) + tuple(held[2:])
    writes = [
        pltpu.make_async_copy(src, dst, sem.at[1, i])
        for i, (src, dst) in enumerate(zip(sources, results))
    ]
    for read in reads:
        read.start()
    if tail:
        dx_held[pl.ds(own, tail), :] = jnp.zeros((tail, dx_held.shape[1]), jnp.bfloat16)
    reads[0].wait()
    reads[1].wait()
    dx_ref[...] = matmul(combine_held[...], dx_held[...]).astype(jnp.bfloat16)
    writes[0].start()
    for read, write in zip(reads[2:], writes[1:]):
        read.wait()
        write.start()
    for write in writes:
        write.wait()


def fused(n, tokens, expert_choice, gate_prob, cotangent, w_gate, w_up, w_down):
    tok, features = tokens.shape
    units = w_gate.shape[1]
    capacity = 3 * tok // (2 * n)
    own = n * capacity
    everyone = 4 * own
    padded = -(-own // LANES) * LANES
    width = features // 4
    bf16, f32 = jnp.bfloat16, jnp.float32
    hbm = pl.BlockSpec(memory_space=pltpu.HBM)
    work = 2 * units * features * (6 * own + 3 * everyone + 3 * own)
    made_out, dx_back, combine, *others = pl.pallas_call(
        functools.partial(kernel, n, capacity),
        out_shape=(
            jax.ShapeDtypeStruct((tok, features), bf16),
            jax.ShapeDtypeStruct((own, features), bf16),
            jax.ShapeDtypeStruct((tok, padded), bf16),
            jax.ShapeDtypeStruct((1, tok), f32),
        )
        + (jax.ShapeDtypeStruct((units, width), bf16),) * 3,
        in_specs=[hbm] * 7,
        out_specs=(hbm,) * 7,
        scratch_shapes=[
            pltpu.VMEM((tok, features), bf16),
            pltpu.VMEM((1, tok), jnp.int32),
            pltpu.VMEM((1, tok), f32),
            pltpu.VMEM((tok, features), bf16),
            pltpu.VMEM((units, features), bf16),
            pltpu.VMEM((units, features), bf16),
            pltpu.VMEM((units, features), bf16),
            pltpu.VMEM((own - capacity, features), bf16),
            pltpu.VMEM((own - capacity, features), bf16),
            pltpu.VMEM((everyone, features), bf16),
            pltpu.VMEM((everyone, features), bf16),
            pltpu.VMEM((own, units), f32),
            pltpu.VMEM((own, units), f32),
            pltpu.VMEM((own, units), bf16),
            pltpu.VMEM((own, units), bf16),
            pltpu.VMEM((own, units), bf16),
            pltpu.VMEM((units, everyone), f32),
            pltpu.VMEM((units, everyone), f32),
            pltpu.VMEM((units, everyone), bf16),
            pltpu.VMEM((own, features), bf16),
            pltpu.VMEM((own, features), bf16),
            pltpu.VMEM((padded, features), bf16),
            pltpu.VMEM((tok, features), bf16),
            pltpu.VMEM((tok, padded), bf16),
            pltpu.VMEM((1, tok), f32),
            pltpu.VMEM((units, width), bf16),
            pltpu.VMEM((units, width), bf16),
            pltpu.VMEM((units, width), bf16),
            pltpu.SemaphoreType.DMA((7,)),
            pltpu.SemaphoreType.DMA((7,)),
            pltpu.SemaphoreType.DMA((2, n)),
            pltpu.SemaphoreType.DMA((2, n)),
            pltpu.SemaphoreType.DMA((2, 3, n)),
            pltpu.SemaphoreType.DMA((2, 3, n)),
            pltpu.SemaphoreType.DMA((2, n)),
            pltpu.SemaphoreType.DMA((2, n)),
        ],
        cost_estimate=pl.CostEstimate(
            flops=work, bytes_accessed=6 * units * features, transcendentals=units * everyone
        ),
        compiler_params=pltpu.CompilerParams(
            collective_id=0, has_side_effects=True, vmem_limit_bytes=60 * 1024 * 1024
        ),
    )(
        tokens,
        expert_choice.reshape(1, tok),
        gate_prob.reshape(1, tok),
        cotangent,
        w_gate[0],
        w_up[0],
        w_down[0],
    )
    finished = jax.ShapeDtypeStruct((tok, features), bf16)
    d_tokens, layer_out, d_gate, *grads = pl.pallas_call(
        write_out,
        out_shape=(finished,)
        + tuple(jax.ShapeDtypeStruct(r.shape, r.dtype) for r in (made_out, *others)),
        in_specs=[hbm] * 7,
        out_specs=(hbm,) * 6,
        scratch_shapes=[pltpu.VMEM((padded, features), bf16)]
        + [pltpu.VMEM(r.shape, r.dtype) for r in (combine, made_out, *others)]
        + [pltpu.VMEM((tok, features), bf16), pltpu.SemaphoreType.DMA((2, 7))],
        compiler_params=pltpu.CompilerParams(vmem_limit_bytes=60 * 1024 * 1024),
    )(dx_back, combine, made_out, *others)
    return (layer_out, d_tokens, d_gate.reshape(tok, 1), *(grad[None] for grad in grads))


def solution(mesh):
    in_specs = (
        P(("parts", "expert", "dp", "sub"), None),
        P(("parts", "expert", "dp", "sub"), None),
        P(("parts", "expert", "dp", "sub"), None),
        P(("parts", "expert", "dp", "sub"), None),
        P("expert", "sub", None),
        P("expert", "sub", None),
        P("expert", "sub", None),
    )
    out_specs = (
        P(("parts", "expert", "dp", "sub"), None),
        P(("parts", "expert", "dp", "sub"), None),
        P(("parts", "expert", "dp", "sub"), None),
        P(("parts", "expert"), "sub", "dp"),
        P(("parts", "expert"), "sub", "dp"),
        P(("parts", "expert"), "sub", "dp"),
    )
    shape = dict(mesh.shape)
    fits = shape["sub"] == 1 and shape["dp"] == 4

    def device_part(tokens, expert_choice, *rest):
        capacity = 3 * tokens.shape[0] // (2 * shape["expert"])
        one_choice = expert_choice.shape[1] == 1
        if fits and one_choice and tokens.shape[0] == LANES and capacity % 16 == 0:
            return fused(shape["expert"], tokens, expert_choice, *rest)
        return local(tokens, expert_choice, *rest)

    return jax.shard_map(device_part, mesh=mesh, in_specs=in_specs, out_specs=out_specs, check_vma=False)
```
